256 devices in a mesh: rep: 16 (over y, z_lo), tp: 16 (over x, z_hi, core).
Axes of the slice: x: 4, y: 4, z: 8 (z_hi: 2, z_lo: 4; z = z_hi * 4 + z_lo), core: 2. Of those that a mesh axis runs over, the one named last changes fastest.
Arguments:
- hidden: bfloat16 [2, 2048, 8192], P(None, 'rep', 'tp'), may hold values from -6 to 6
- query_base_weight: bfloat16 [8192, 4096], P(None, 'tp'), may hold values from -0.0625 to 0.0625
- output_base_weight: bfloat16 [4096, 8192], P('tp'), may hold values from -0.09375 to 0.09375
- cache: bfloat16 [2048, 16, 32, 256], P('rep', 'tp'), may hold values from -310 to 310, as said below
- fresh: bfloat16 [2048, 16, 2, 256], P('rep', 'tp'), may hold values from -4 to 4, as said below
- lengths: int32 [2048], P('rep'), may hold values from 2 to 32, as said below
- grad_query_down: float32 [16, 64, 8192], P('rep', None, 'tp'), may hold values from -20000 to 20000
- grad_query_up: float32 [16, 64, 4096], P('rep', None, 'tp'), may hold values from -20000 to 20000
- grad_output_down: float32 [16, 64, 4096], P('rep', None, 'tp'), may hold values from -20000 to 20000
- grad_output_up: float32 [16, 64, 8192], P('rep', None, 'tp'), may hold values from -20000 to 20000
- ask_left_matrix: float32 [64, 8192], P('rep', 'tp'), may hold values from -0.0625 to 0.0625
- ask_right_matrix: float32 [64, 4096], P('rep', 'tp'), may hold values from -0.375 to 0.375
- proj_left_matrix: float32 [64, 4096], P('rep', 'tp'), may hold values from -0.09375 to 0.09375
- proj_right_matrix: float32 [64, 8192], P('rep', 'tp'), may hold values from -0.375 to 0.375
- mean_gradient_ask_left: float32 [64, 8192], P('rep', 'tp'), may hold values from -6 to 6
- mean_gradient_ask_right: float32 [64, 4096], P('rep', 'tp'), may hold values from -6 to 6
- mean_gradient_proj_left: float32 [64, 4096], P('rep', 'tp'), may hold values from -6 to 6
- mean_gradient_proj_right: float32 [64, 8192], P('rep', 'tp'), may hold values from -6 to 6
- variance_ask_left: float32 [64, 8192], P('rep', 'tp'), may hold values from 0.25 to 4
- variance_ask_right: float32 [64, 4096], P('rep', 'tp'), may hold values from 0.25 to 4
- variance_proj_left: float32 [64, 4096], P('rep', 'tp'), may hold values from 0.25 to 4
- variance_proj_right: float32 [64, 8192], P('rep', 'tp'), may hold values from 0.25 to 4
Outputs:
- decoded: bfloat16 [2, 2048, 8192], P(None, 'rep', 'tp')
- next_query_down: float32 [64, 8192], P('rep', 'tp')
- next_query_up: float32 [64, 4096], P('rep', 'tp')
- next_output_down: float32 [64, 4096], P('rep', 'tp')
- next_output_up: float32 [64, 8192], P('rep', 'tp')
- next_moment_query_down: float32 [64, 8192], P('rep', 'tp')
- next_moment_query_up: float32 [64, 4096], P('rep', 'tp')
- next_moment_output_down: float32 [64, 4096], P('rep', 'tp')
- next_moment_output_up: float32 [64, 8192], P('rep', 'tp')
- next_square_query_down: float32 [64, 8192], P('rep', 'tp')
- next_square_query_up: float32 [64, 4096], P('rep', 'tp')
- next_square_output_down: float32 [64, 4096], P('rep', 'tp')
- next_square_output_up: float32 [64, 8192], P('rep', 'tp')
The draws below stay inside these ranges and needn't reach their ends.
Inputs may be any that keep to these rules, and one draw needn't show every extreme that they name: `lengths`: every rollout group's block of 128 rows holds a row with 32 filled slots. `cache`: tensor ranks whose query heads share a key-value head hold equal copies. `fresh`: tensor ranks whose query heads share a key-value head hold equal copies.
All inputs are finite; a program needn't handle non-finite values.
Results may differ from the reference program's by a relative error of at most 0.011.
Values may be sent and summed in bfloat16 or wider, within the bound.
No kernel may reach another device: no remote copies, remote signals or barrier semaphores. Data moves between devices by JAX's collectives and lax.ppermute only.
A program may use at most 128 MiB of HBM per device.

```python
import math
from functools import partial
import jax
import jax.numpy as jnp
from jax import lax

MODEL_WIDTH = 8192
HEAD_SPAN = 128
ATTN_HEADS_HALF = 32
KVH = 4
LOW_DIMENSION = 64
ALPHA_DIVIDEND = 32
CACHE = 32
ROWS = 128
WINDOW_QCOLS = 4096
ROWS_ALL = 2048
PARAMS = 1572864
N_REP = 16
N_TP = 16


def crude_derivatives(key, row_count, column_count, magnitude):
    key_noise = jax.random.fold_in(key, 0)
    key_rows = jax.random.fold_in(key, 2)
    key_cols = jax.random.fold_in(key, 3)
    noise_draw = jnp.clip(jax.random.normal(key_noise, (N_REP, row_count, column_count), jnp.float32), -5.0, 5.0)
    blended = noise_draw
    row_scale = jnp.exp(jax.random.uniform(key_rows, (1, row_count, 1), jnp.float32) * math.log(10.0))
    col_scale = jnp.exp(jax.random.uniform(key_cols, (1, 1, column_count), jnp.float32) * math.log(10.0))
    rep_pos = jnp.arange(N_REP, dtype=jnp.float32).reshape(N_REP, 1, 1) / max(N_REP - 1, 1)
    row_pos = jnp.arange(row_count, dtype=jnp.float32).reshape(1, row_count, 1) / max(row_count - 1, 1)
    col_pos = jnp.arange(column_count, dtype=jnp.float32).reshape(1, 1, column_count) / max(column_count - 1, 1)
    rising = jnp.exp(math.log(3.0) * (rep_pos + row_pos + col_pos))
    return blended * row_scale * col_scale * rising * magnitude


def draw_grad_query_down(key, part):
    key = jax.random.fold_in(key, 31)
    return crude_derivatives(key, LOW_DIMENSION, MODEL_WIDTH, 0.05)


def draw_grad_query_up(key, part):
    key = jax.random.fold_in(key, 32)
    return crude_derivatives(key, LOW_DIMENSION, ATTN_HEADS_HALF * HEAD_SPAN, 0.05)


def draw_grad_output_down(key, part):
    key = jax.random.fold_in(key, 33)
    return crude_derivatives(key, LOW_DIMENSION, ATTN_HEADS_HALF * HEAD_SPAN, 0.05)


def draw_grad_output_up(key, part):
    key = jax.random.fold_in(key, 34)
    return crude_derivatives(key, LOW_DIMENSION, MODEL_WIDTH, 0.05)


def draw_cache(key, part):
    key = jax.random.fold_in(key, 21)
    key_base = jax.random.fold_in(key, 0)
    sampled = jnp.clip(jax.random.normal(key_base, (ROWS * N_REP, KVH, CACHE, 2 * HEAD_SPAN), jnp.float32), -4.0, 4.0)
    return jnp.repeat(sampled, N_TP // KVH, axis=1).astype(jnp.bfloat16)


def draw_fresh(key, part):
    key = jax.random.fold_in(key, 22)
    sampled = jnp.clip(jax.random.normal(key, (ROWS * N_REP, KVH, 2, 2 * HEAD_SPAN), jnp.float32), -4.0, 4.0)
    return jnp.repeat(sampled, N_TP // KVH, axis=1).astype(jnp.bfloat16)


def draw_lengths(key, part):
    key = jax.random.fold_in(key, 23)
    sampled = jax.random.randint(key, (ROWS * N_REP,), 2, CACHE + 1, dtype=jnp.int32)
    first_rows = jnp.arange(ROWS * N_REP, dtype=jnp.int32) % ROWS == 0
    return jnp.where(first_rows, CACHE, sampled).astype(jnp.int32)


def steps_of(own_key, extent, pieces, smallest, top_value):
    factor_of = 1.0
    for position, parts in pieces:
        draws = jax.random.uniform(jax.random.fold_in(jax.random.fold_in(own_key, 6), position), (parts,), jnp.float32, smallest / len(pieces), top_value / len(pieces))
        factor_of = factor_of * jnp.repeat(jnp.exp(draws), extent[position] // parts).reshape((-1,) + (1,) * (len(extent) - 1 - position))
    return factor_of


def noise(own_key, shape, scale, bound, cuts=(), held_as=jnp.bfloat16):
    result = jax.random.normal(own_key, shape, jnp.float32) * scale
    if len(cuts) > 0:
        result = steps_of(own_key, shape, cuts, -0.22, 0.18) * result
    return jnp.clip(result, min=-bound, max=bound).astype(held_as)


def setup_inputs(seed: int = 0) -> dict:
    splits = jax.random.split(jax.random.key(seed), 23)
    return {
        "hidden": noise(splits[0], (2, ROWS_ALL, MODEL_WIDTH), 1.0, 6.0, ((1, 16), (2, 16))),
        "query_base_weight": noise(splits[1], (MODEL_WIDTH, WINDOW_QCOLS), MODEL_WIDTH ** -0.5, 0.0625, ((1, 16),)),
        "output_base_weight": noise(splits[2], (WINDOW_QCOLS, MODEL_WIDTH), WINDOW_QCOLS ** -0.5, 0.09375, ((0, 16),)),
        "cache": draw_cache(jax.random.fold_in(splits[22], 71), 0),
        "fresh": draw_fresh(jax.random.fold_in(splits[22], 71), 0),
        "lengths": draw_lengths(jax.random.fold_in(splits[22], 71), 0),
        "grad_query_down": draw_grad_query_down(jax.random.fold_in(splits[22], 71), 0),
        "grad_query_up": draw_grad_query_up(jax.random.fold_in(splits[22], 71), 0),
        "grad_output_down": draw_grad_output_down(jax.random.fold_in(splits[22], 71), 0),
        "grad_output_up": draw_grad_output_up(jax.random.fold_in(splits[22], 71), 0),
        "ask_left_matrix": noise(splits[10], (LOW_DIMENSION, MODEL_WIDTH), MODEL_WIDTH ** -0.5, 0.0625, ((0, 16), (1, 16)), jnp.float32),
        "ask_right_matrix": noise(splits[11], (LOW_DIMENSION, WINDOW_QCOLS), (4 * LOW_DIMENSION) ** -0.5, 0.375, ((0, 16), (1, 16)), jnp.float32),
        "proj_left_matrix": noise(splits[12], (LOW_DIMENSION, WINDOW_QCOLS), WINDOW_QCOLS ** -0.5, 0.09375, ((0, 16), (1, 16)), jnp.float32),
        "proj_right_matrix": noise(splits[13], (LOW_DIMENSION, MODEL_WIDTH), (4 * LOW_DIMENSION) ** -0.5, 0.375, ((0, 16), (1, 16)), jnp.float32),
        "mean_gradient_ask_left": noise(splits[14], (LOW_DIMENSION, MODEL_WIDTH), 1.0, 6.0, ((0, 16), (1, 16)), jnp.float32),
        "mean_gradient_ask_right": noise(splits[15], (LOW_DIMENSION, WINDOW_QCOLS), 1.0, 6.0, ((0, 16), (1, 16)), jnp.float32),
        "mean_gradient_proj_left": noise(splits[16], (LOW_DIMENSION, WINDOW_QCOLS), 1.0, 6.0, ((0, 16), (1, 16)), jnp.float32),
        "mean_gradient_proj_right": noise(splits[17], (LOW_DIMENSION, MODEL_WIDTH), 1.0, 6.0, ((0, 16), (1, 16)), jnp.float32),
        "variance_ask_left": jnp.clip(jnp.exp(math.log(4.0) - 2.7725887 * jax.random.uniform(splits[18], (LOW_DIMENSION, MODEL_WIDTH), jnp.float32) ** steps_of(splits[18], (LOW_DIMENSION, MODEL_WIDTH), ((0, 16), (1, 16)), -0.2, 0.2)), 0.25, 4.0),
        "variance_ask_right": jnp.clip(jnp.exp(math.log(4.0) - 2.7725887 * jax.random.uniform(splits[19], (LOW_DIMENSION, WINDOW_QCOLS), jnp.float32) ** steps_of(splits[19], (LOW_DIMENSION, WINDOW_QCOLS), ((0, 16), (1, 16)), -0.2, 0.2)), 0.25, 4.0),
        "variance_proj_left": jnp.clip(jnp.exp(math.log(4.0) - 2.7725887 * jax.random.uniform(splits[20], (LOW_DIMENSION, WINDOW_QCOLS), jnp.float32) ** steps_of(splits[20], (LOW_DIMENSION, WINDOW_QCOLS), ((0, 16), (1, 16)), -0.2, 0.2)), 0.25, 4.0),
        "variance_proj_right": jnp.clip(jnp.exp(math.log(4.0) - 2.7725887 * jax.random.uniform(splits[21], (LOW_DIMENSION, MODEL_WIDTH), jnp.float32) ** steps_of(splits[21], (LOW_DIMENSION, MODEL_WIDTH), ((0, 16), (1, 16)), -0.2, 0.2)), 0.25, 4.0),
    }


beta_one = 0.9
beta_two = 0.999
bias_one = 1.0 - math.exp(1000.0 * math.log(0.9))
bias_two = 1.0 - math.exp(1000.0 * math.log(0.999))
adam_eps = 1e-08
learn_rate = 0.005
norm_eps = 1e-06
rope_base = 1000000.0

def adam_update(factor, gradient, moment, square, clip_factor):
    scaled = clip_factor * gradient
    moment_new = beta_one * moment + (1.0 - beta_one) * scaled
    square_new = beta_two * square + (1.0 - beta_two) * scaled * scaled
    update = moment_new / bias_one / (jnp.sqrt(square_new / bias_two) + adam_eps)
    return (factor - learn_rate * update, moment_new, square_new)

def rotate_heads(queries, positions):
    half_size = queries.shape[-1] // 2
    frequency = jnp.power(rope_base, -2.0 * jnp.arange(half_size, dtype=jnp.float32) / queries.shape[-1])
    angles = positions.astype(jnp.float32)[:, None] * frequency[None, :]
    cosine = jnp.cos(angles)[:, None, :]
    sine_part = jnp.sin(angles)[:, None, :]
    lower_half = queries[..., :half_size]
    upper_half = queries[..., half_size:]
    return jnp.concatenate([lower_half * cosine - upper_half * sine_part, upper_half * cosine + lower_half * sine_part], axis=-1)

def attend(queries, cache_rows, fresh_rows, row_lengths, offset):
    row_count = queries.shape[0]
    head_count = queries.shape[1] // HEAD_SPAN
    rotated = rotate_heads(queries.reshape(row_count, head_count, HEAD_SPAN), row_lengths + offset)
    scaled = (rotated * (1.0 / math.sqrt(HEAD_SPAN))).astype(jnp.bfloat16).astype(jnp.float32)
    key_part = cache_rows[:, :, :HEAD_SPAN].astype(jnp.float32)
    value_part = cache_rows[:, :, HEAD_SPAN:].astype(jnp.float32)
    fresh_part = fresh_rows[:, :offset + 1].astype(jnp.float32)
    scores = jnp.einsum('rhd,rcd->rhc', scaled, key_part)
    live_mask = jnp.arange(cache_rows.shape[1])[None, :] < row_lengths[:, None]
    scores = jnp.where(live_mask[:, None, :], scores, -1e+30)
    fresh_scores = jnp.einsum('rhd,rjd->rhj', scaled, fresh_part[:, :, :HEAD_SPAN])
    row_max = jnp.maximum(lax.optimization_barrier(jnp.max(scores, axis=-1)), lax.optimization_barrier(jnp.max(fresh_scores, axis=-1)))[..., None]
    cache_exp = jnp.exp(scores - row_max)
    fresh_exp = jnp.exp(fresh_scores - row_max)
    denominator = lax.optimization_barrier(jnp.sum(cache_exp, axis=-1, keepdims=True)) + lax.optimization_barrier(jnp.sum(fresh_exp, axis=-1, keepdims=True))
    cache_weights = (cache_exp / denominator).astype(jnp.bfloat16).astype(jnp.float32)
    fresh_weights = (fresh_exp / denominator).astype(jnp.bfloat16).astype(jnp.float32)
    attended = jnp.einsum('rhc,rcd->rhd', cache_weights, value_part) + jnp.einsum('rhj,rjd->rhd', fresh_weights, fresh_part[:, :, HEAD_SPAN:])
    return attended.reshape(row_count, head_count * HEAD_SPAN).astype(jnp.bfloat16)

def reference(hidden, query_base_weight, output_base_weight, cache, fresh, lengths, grad_query_down, grad_query_up, grad_output_down, grad_output_up, ask_left_matrix, ask_right_matrix, proj_left_matrix, proj_right_matrix, mean_gradient_ask_left, mean_gradient_ask_right, mean_gradient_proj_left, mean_gradient_proj_right, variance_ask_left, variance_ask_right, variance_proj_left, variance_proj_right):
    gradients = (lax.optimization_barrier(jnp.sum(grad_query_down, axis=0)), lax.optimization_barrier(jnp.sum(grad_query_up, axis=0)), lax.optimization_barrier(jnp.sum(grad_output_down, axis=0)), lax.optimization_barrier(jnp.sum(grad_output_up, axis=0)))
    total_squares = jnp.sum(gradients[0] * gradients[0]) + jnp.sum(gradients[1] * gradients[1]) + jnp.sum(gradients[2] * gradients[2]) + jnp.sum(gradients[3] * gradients[3])
    clip_factor = jnp.minimum(1.0, math.sqrt(PARAMS) / (jnp.sqrt(total_squares) + norm_eps))
    factors = (ask_left_matrix, ask_right_matrix, proj_left_matrix, proj_right_matrix)
    moments = (mean_gradient_ask_left, mean_gradient_ask_right, mean_gradient_proj_left, mean_gradient_proj_right)
    squares = (variance_ask_left, variance_ask_right, variance_proj_left, variance_proj_right)
    updated = [adam_update(factors[index], gradients[index], moments[index], squares[index], clip_factor) for index in range(4)]
    factor_copies = [entry[0].astype(jnp.bfloat16) for entry in updated]
    delta_multiplier = ALPHA_DIVIDEND / LOW_DIMENSION
    contract_pair = (((0,), (0,)), ((), ()))
    merged_query_weight = (query_base_weight.astype(jnp.float32) + delta_multiplier * lax.dot_general(factor_copies[0], factor_copies[1], contract_pair, preferred_element_type=jnp.float32)).astype(jnp.bfloat16)
    merged_output_weight = (output_base_weight.astype(jnp.float32) + delta_multiplier * lax.dot_general(factor_copies[2], factor_copies[3], contract_pair, preferred_element_type=jnp.float32)).astype(jnp.bfloat16)
    heads_local = ATTN_HEADS_HALF // N_TP
    groups = (jnp.moveaxis(hidden.reshape(2, N_REP, ROWS, MODEL_WIDTH), 1, 0), cache.reshape(N_REP, ROWS, N_TP, CACHE, 2 * HEAD_SPAN), fresh.reshape(N_REP, ROWS, N_TP, 2, 2 * HEAD_SPAN), lengths.reshape(N_REP, ROWS))

    def decode_group(block):
        inputs, cache_rows, fresh_rows, row_lengths = block
        results = []
        for offset in range(2):
            queries = jnp.dot(inputs[offset], merged_query_weight, preferred_element_type=jnp.float32)
            queries = queries.reshape(ROWS, N_TP, heads_local * HEAD_SPAN)
            attended = jax.vmap(partial(attend, offset=offset), in_axes=(1, 1, 1, None), out_axes=1)(queries, cache_rows, fresh_rows, row_lengths)
            attended = attended.reshape(ROWS, ATTN_HEADS_HALF * HEAD_SPAN)
            summed_out = jnp.dot(attended, merged_output_weight, preferred_element_type=jnp.float32)
            results.append((inputs[offset].astype(jnp.float32) + summed_out).astype(jnp.bfloat16))
        return jnp.stack(results)
    decoded = lax.map(decode_group, groups)
    decoded = jnp.moveaxis(decoded, 0, 1).reshape(2, N_REP * ROWS, MODEL_WIDTH)
    return (decoded, updated[0][0], updated[1][0], updated[2][0], updated[3][0], updated[0][1], updated[1][1], updated[2][1], updated[3][1], updated[0][2], updated[1][2], updated[2][2], updated[3][2])
```

```python
import math

import jax
import jax.numpy as jnp
from jax import lax
from jax.experimental import pallas as pl
from jax.experimental.pallas import tpu as pltpu
from jax.sharding import PartitionSpec as P

HEAD = 128
PARAMS = 1572864
N = 16

beta_one = 0.9
beta_two = 0.999
bias_one = 1.0 - math.exp(1000.0 * math.log(0.9))
bias_two = 1.0 - math.exp(1000.0 * math.log(0.999))
adam_eps = 1e-08
learn_rate = 0.005
norm_eps = 1e-06
rope_base = 1000000.0

bf16 = jnp.bfloat16
f32 = jnp.float32


def adam_update(factor, gradient, moment, square, clip_factor):
    scaled = clip_factor * gradient
    moment_new = beta_one * moment + (1.0 - beta_one) * scaled
    square_new = beta_two * square + (1.0 - beta_two) * scaled * scaled
    update = moment_new / bias_one / (jnp.sqrt(square_new / bias_two) + adam_eps)
    return (factor - learn_rate * update, moment_new, square_new)


def shift(value, move):
    return lax.ppermute(value, "tp", [(i, move(i)) for i in range(N)])


def to_core(value):
    return shift(value, lambda i: i ^ 1)


def to_z(value):
    return shift(value, lambda i: i ^ 2)


def to_right(value):
    return shift(value, lambda i: (i + 4) % N)


def to_left(value):
    return shift(value, lambda i: (i + 12) % N)


def give_all(value, axis):
    wide = lax.optimization_barrier(jnp.broadcast_to(value[None], (N,) + value.shape))
    return lax.all_to_all(wide, axis, 0, 0)


def dot(a, b, contract=((1,), (0,))):
    return lax.dot_general(a, b, (contract, ((), ())), preferred_element_type=f32)


def base_kernel(order, mine, other, w_mine, w_other, out):
    @pl.when(pl.program_id(0) == 0)
    def _():
        out[...] = jnp.zeros_like(out)

    out[...] += dot(mine[0], w_mine[0]) + dot(other[0], w_other[0])


def base_queries(order, mine, other, weight):
    weight = weight.reshape(N, 512, 256)
    return pl.pallas_call(
        base_kernel,
        grid_spec=pltpu.PrefetchScalarGridSpec(
            num_scalar_prefetch=1,
            grid=(8,),
            in_specs=[
                pl.BlockSpec((1, 256, 512), lambda k, o: (k, 0, 0)),
                pl.BlockSpec((1, 256, 512), lambda k, o: (k, 0, 0)),
                pl.BlockSpec((1, 512, 256), lambda k, o: (o[k], 0, 0)),
                pl.BlockSpec((1, 512, 256), lambda k, o: (o[k + 8], 0, 0)),
            ],
            out_specs=pl.BlockSpec((256, 256), lambda k, o: (0, 0)),
        ),
        out_shape=jax.ShapeDtypeStruct((256, 256), f32),
        cost_estimate=pl.CostEstimate(
            flops=2 * 256 * 8192 * 256, bytes_accessed=8 << 20, transcendentals=0
        ),
    )(order, mine, other, weight, weight)


ROWS = 16


def attend_kernel(base, low, up, cosine, sine, lens, cache, fresh, out):
    half = pl.program_id(0)
    base_row = pl.multiple_of(half * ROWS, ROWS)
    lows = jnp.sum(low[:, 0].astype(f32), axis=0).astype(bf16)
    ups = up[...]
    zero = jnp.zeros_like(ups)
    pieces = []
    for step in range(2):
        both = jnp.concatenate([ups, zero] if step == 0 else [zero, ups], axis=0)
        query = base[step] + 0.5 * dot(lows, both)
        for head in range(2):
            one = query[:, head * HEAD : (head + 1) * HEAD]
            turned = one * cosine[step] + pltpu.roll(one, HEAD // 2, 1) * sine[step]
            pieces.append((turned * (1.0 / math.sqrt(HEAD))).astype(bf16))
    queries = jnp.concatenate(pieces, axis=0)
    keys = cache[:, :HEAD]
    values = cache[:, HEAD:]
    new_keys = fresh[:, :HEAD]
    new_values = fresh[:, HEAD:]
    scores = dot(queries, keys, ((1,), (1,)))
    new_scores = dot(queries, new_keys, ((1,), (1,)))
    slots = lax.broadcasted_iota(jnp.int32, scores.shape, 1)
    rows = lax.broadcasted_iota(jnp.int32, scores.shape, 0) & (ROWS - 1)
    length = jnp.concatenate([lens[...]] * 4, axis=0)
    length = jnp.concatenate([length] * (scores.shape[1] // HEAD), axis=1)
    live = ((slots >> 5) == rows) & ((slots & 31) < length)
    scores = jnp.where(live, scores, -1e30)
    new_slots = lax.broadcasted_iota(jnp.int32, new_scores.shape, 1)
    new_index = lax.broadcasted_iota(jnp.int32, new_scores.shape, 0)
    new_live = ((new_slots >> 1) == (new_index & (ROWS - 1))) & (
        (new_slots & 1) <= (new_index >> 5)
    )
    new_scores = jnp.where(new_live, new_scores, -1e30)
    top = jnp.maximum(
        jnp.max(scores, axis=1, keepdims=True), jnp.max(new_scores, axis=1, keepdims=True)
    )
    weights = jnp.exp(scores - top)
    new_weights = jnp.exp(new_scores - top)
    total = jnp.sum(weights, axis=1, keepdims=True) + jnp.sum(new_weights, axis=1, keepdims=True)
    inverse = 1.0 / total
    result = dot((weights * inverse).astype(bf16), values)
    result = result + dot((new_weights * inverse).astype(bf16), new_values)
    for step in range(2):
        for head in range(2):
            at = (step * 2 + head) * ROWS
            out[step, :, head * HEAD : (head + 1) * HEAD] = result[at : at + ROWS].astype(bf16)


def attention(base, low, up, cosine, sine, lens, cache, fresh):
    return pl.pallas_call(
        attend_kernel,
        grid=(128 // ROWS,),
        in_specs=[
            pl.BlockSpec((2, ROWS, 256), lambda k: (0, k, 0)),
            pl.BlockSpec((N, 1, ROWS, 128), lambda k: (0, 0, k, 0)),
            pl.BlockSpec((64, 256), lambda k: (0, 0)),
            pl.BlockSpec((2, ROWS, 128), lambda k: (0, k, 0)),
            pl.BlockSpec((2, ROWS, 128), lambda k: (0, k, 0)),
            pl.BlockSpec((ROWS, 128), lambda k: (k, 0)),
            pl.BlockSpec((ROWS * 32, 256), lambda k: (k, 0)),
            pl.BlockSpec((ROWS * 2, 256), lambda k: (k, 0)),
        ],
        out_specs=pl.BlockSpec((2, ROWS, 256), lambda k: (0, k, 0)),
        out_shape=jax.ShapeDtypeStruct((2, 128, 256), bf16),
        cost_estimate=pl.CostEstimate(
            flops=2 * 512 * 512 * 256, bytes_accessed=3 << 20, transcendentals=512 * 512
        ),
    )(base, low, up, cosine, sine, lens, cache, fresh)


def project_kernel(order, mine, other, w_mine, w_other, out):
    out[0] = (dot(mine[...], w_mine[...]) + dot(other[...], w_other[...])).astype(bf16)


def project(order, mine, other, w_mine, w_other):
    return pl.pallas_call(
        project_kernel,
        grid_spec=pltpu.PrefetchScalarGridSpec(
            num_scalar_prefetch=1,
            grid=(8,),
            in_specs=[
                pl.BlockSpec((256, 256), lambda k, o: (0, 0)),
                pl.BlockSpec((256, 256), lambda k, o: (0, 0)),
                pl.BlockSpec((256, 512), lambda k, o: (0, o[k])),
                pl.BlockSpec((256, 512), lambda k, o: (0, o[k] // 2)),
            ],
            out_specs=pl.BlockSpec((1, 256, 512), lambda k, o: (k, 0, 0)),
        ),
        out_shape=jax.ShapeDtypeStruct((8, 256, 512), bf16),
        cost_estimate=pl.CostEstimate(
            flops=2 * 256 * 512 * 4096, bytes_accessed=6 << 20, transcendentals=0
        ),
    )(order, mine, other, w_mine, w_other)


def on_device(
    hidden,
    query_base_weight,
    output_base_weight,
    cache,
    fresh,
    lengths,
    grad_query_down,
    grad_query_up,
    grad_output_down,
    grad_output_up,
    *state,
):
    widths = (512, 256, 256, 512)
    cuts = (512, 768, 1024)
    rank = lax.axis_index("tp")
    core = rank % 2
    z_hi = (rank // 2) % 2
    x = rank // 4

    order = jnp.stack(
        [
            ((x + dx) % 4) * 4 + (z_hi ^ dz) * 2 + core
            for dx in (0, 1, 2, 3)
            for dz in (0, 1)
        ]
    ).astype(jnp.int32)
    orders = jnp.concatenate([order, order ^ 1])

    gradient = jnp.concatenate(
        [grad_query_down[0], grad_query_up[0], grad_output_down[0], grad_output_up[0]], axis=1
    ).reshape(N, 4, 1536)
    summed = jnp.sum(lax.all_to_all(gradient, "rep", 0, 0), axis=0)

    zed = to_z(hidden)
    pair = jnp.stack([hidden, zed])
    left = to_right(pair)
    right = to_left(pair)

    factor = jnp.concatenate(state[0:4], axis=1)
    moment = jnp.concatenate(state[4:8], axis=1)
    square = jnp.concatenate(state[8:12], axis=1)
    whole = lax.all_gather(
        jnp.concatenate([factor, moment, square], axis=1).reshape(8, 2304), "rep", axis=0
    ).reshape(N, 4, 3, 1536)

    squares = jnp.sum(summed * summed)
    high = squares.astype(bf16)
    low = (squares - high.astype(f32)).astype(bf16)
    tail = jnp.where(
        lax.broadcasted_iota(jnp.int32, (4, 128), 0) == 0, high, low
    )
    sent = jnp.concatenate([summed.astype(bf16), tail], axis=1)
    all_summed = give_all(sent, "rep")
    own_squares = jnp.sum(all_summed[:, 0:2, 1536].astype(f32))

    far_a = to_right(left[:, 0])
    far_b = to_left(right[:, 1])
    far = jnp.stack([far_a, far_b], axis=1)
    mine = jnp.stack([pair, right, far, left]).reshape(8, 256, 512)
    other = to_core(mine)

    total_squares = jnp.sum(give_all(jnp.full((1, 128), own_squares), "tp")[:, 0, 0])
    clip_factor = jnp.minimum(1.0, math.sqrt(PARAMS) / (jnp.sqrt(total_squares) + norm_eps))

    base = base_queries(orders, mine, other, query_base_weight).reshape(2, 128, 256)

    copies, _, _ = adam_update(
        whole[:, :, 0],
        all_summed[:, :, :1536].astype(f32),
        whole[:, :, 1],
        whole[:, :, 2],
        clip_factor,
    )
    copies = copies.astype(bf16).reshape(64, 1536)
    down, up, out_down, out_up = jnp.split(copies, cuts, axis=1)

    low_part = jnp.concatenate(
        [dot(hidden[0], down, ((1,), (1,))), dot(hidden[1], down, ((1,), (1,)))], axis=1
    ).astype(bf16)
    lows = give_all(low_part[None], "tp")

    updated, moved, squared = adam_update(factor, summed, moment, square, clip_factor)

    exponents = -2.0 * jnp.arange(64, dtype=f32) / HEAD
    frequency = jnp.power(rope_base, exponents)
    positions = (lengths[None, :] + jnp.arange(2, dtype=jnp.int32)[:, None]).astype(f32)
    angles = positions[:, :, None] * frequency
    cosine = jnp.cos(angles)
    sine = jnp.sin(angles)
    cosine = jnp.concatenate([cosine, cosine], axis=2)
    sine = jnp.concatenate([-sine, sine], axis=2)
    lens = jnp.broadcast_to(lengths[:, None], (128, 128))
    attended = attention(
        base, lows, up, cosine, sine, lens, cache.reshape(4096, 256), fresh.reshape(256, 256)
    ).reshape(256, 256)

    blocks = output_base_weight.reshape(256, 8, 2, 512)
    give = lax.dynamic_index_in_dim(blocks, 1 - core, 2, keepdims=False).reshape(256, 4096)
    taken = to_core(give)
    attended_other = to_core(attended)
    partial = project(order, attended, attended_other, output_base_weight, taken)
    partial = partial.reshape(4, 2, 2, 128, 512)

    inner = dot(attended, out_down, ((1,), (1,)))
    inner = jnp.concatenate([inner[:128], inner[128:]], axis=1).astype(bf16)
    inner = jnp.sum(give_all(inner, "tp").astype(f32), axis=0).astype(bf16)
    inner = jnp.concatenate([inner[:, :64], inner[:, 64:]], axis=0)

    from_left = to_right(partial[2, :, 0])
    from_right = to_left(partial[2, :, 1])
    go_right = jnp.stack(
        [(partial[1, :, 0].astype(f32) + from_left.astype(f32)).astype(bf16), partial[1, :, 1]],
        axis=1,
    )
    go_left = jnp.stack(
        [partial[3, :, 0], (partial[3, :, 1].astype(f32) + from_right.astype(f32)).astype(bf16)],
        axis=1,
    )
    sums = (
        partial[0].astype(f32) + to_right(go_right).astype(f32) + to_left(go_left).astype(f32)
    )
    from_z = to_z(sums[1].astype(bf16))
    decoded = (
        hidden.astype(f32)
        + sums[0]
        + from_z.astype(f32)
        + 0.5 * dot(inner, out_up).reshape(2, 128, 512)
    ).astype(bf16)

    return (
        decoded,
        *jnp.split(updated, cuts, axis=1),
        *jnp.split(moved, cuts, axis=1),
        *jnp.split(squared, cuts, axis=1),
    )


def solution(mesh):
    return jax.shard_map(
        on_device,
        mesh=mesh,
        in_specs=(
            P(None, "rep", "tp"),
            P(None, "tp"),
            P("tp", None),
            P("rep", "tp", None, None),
            P("rep", "tp", None, None),
            P("rep"),
        )
        + (P("rep", None, "tp"),) * 4
        + (P("rep", "tp"),) * 12,
        out_specs=(P(None, "rep", "tp"),) + (P("rep", "tp"),) * 12,
        check_vma=False,
    )
```

```python
import functools
import math

import jax
import jax.numpy as jnp
from jax import lax
from jax.experimental import pallas as pl
from jax.experimental.pallas import tpu as pltpu
from jax.sharding import PartitionSpec as P

HEAD = 128
PARAMS = 1572864
N = 16

beta_one = 0.9
beta_two = 0.999
bias_one = 1.0 - math.exp(1000.0 * math.log(0.9))
bias_two = 1.0 - math.exp(1000.0 * math.log(0.999))
adam_eps = 1e-08
learn_rate = 0.005
norm_eps = 1e-06
rope_base = 1000000.0

bf16 = jnp.bfloat16
f32 = jnp.float32


def adam_update(factor, gradient, moment, square, clip_factor):
    scaled = clip_factor * gradient
    moment_new = beta_one * moment + (1.0 - beta_one) * scaled
    square_new = beta_two * square + (1.0 - beta_two) * scaled * scaled
    update = moment_new / bias_one / (jnp.sqrt(square_new / bias_two) + adam_eps)
    return (factor - learn_rate * update, moment_new, square_new)


def shift(value, move):
    return lax.ppermute(value, "tp", [(i, move(i)) for i in range(N)])


def to_core(value):
    return shift(value, lambda i: i ^ 1)


def to_z(value):
    return shift(value, lambda i: i ^ 2)


def to_replica(value, bit):
    return lax.ppermute(value, "rep", [(i, i ^ bit) for i in range(N)])


def to_right(value):
    return shift(value, lambda i: (i + 4) % N)


def to_left(value):
    return shift(value, lambda i: (i + 12) % N)


def dot(a, b, contract=((1,), (0,))):
    return lax.dot_general(a, b, (contract, ((), ())), preferred_element_type=f32)


VMEM = pl.BlockSpec(memory_space=pltpu.VMEM)
SMEM = pl.BlockSpec(memory_space=pltpu.SMEM)
ANY = pl.BlockSpec(memory_space=pl.ANY)
HBM = pl.BlockSpec(memory_space=pltpu.HBM)
LARGE, SMALL = 60 << 20, 24 << 20
CHAIN = 48 << 20
WIDTHS = (512, 256, 256, 512)
BLOCKS = [(i, c) for i, w in enumerate(WIDTHS) for c in range(0, w, HEAD)]


class Fetched:
    def __init__(self, copy, ref):
        self.copy, self.ref, self.waited = copy, ref, False

    def there(self):
        if not self.waited:
            self.copy.wait()
            self.waited = True
        return self.ref

    def __getitem__(self, index):
        return self.there()[index]


def call(kernel, shapes, *args, scalars=0, fetch=(), take=(), tokens=(), room=(), limit=LARGE, flops=0, moved=1 << 20):
    out = [jax.ShapeDtypeStruct(s, d) for s, d in shapes]
    single = len(out) == 1
    parts = [f if isinstance(f, tuple) else (f, f.shape, None) for f in (*fetch, *take)]
    first, count = len(args), len(args) + len(parts)
    skip = count + len(tokens)

    def body(*refs):
        ins, outs = refs[:count], refs[skip : skip + len(out)]
        scratch = refs[skip + len(out) :]
        held = []
        for i, (_, _, view) in enumerate(parts):
            source = ins[first + i]
            if view is not None:
                source = view(source, *ins[:scalars])
            copy = pltpu.make_async_copy(source, scratch[i], scratch[len(parts)].at[i])
            copy.start()
            held.append(Fetched(copy, scratch[i]))
        kernel(*ins[:first], *held, *outs, *scratch[len(scratch) - len(room) :])
        for one in held:
            one.there()

    return pl.pallas_call(
        body,
        in_specs=[SMEM] * scalars
        + [VMEM] * (first - scalars)
        + [HBM] * len(fetch)
        + [ANY] * (len(take) + len(tokens)),
        out_specs=VMEM if single else [VMEM] * len(out),
        out_shape=out[0] if single else out,
        scratch_shapes=[pltpu.VMEM(shape, one.dtype) for one, shape, _ in parts]
        + ([pltpu.SemaphoreType.DMA((len(parts),))] if parts else [])
        + list(room),
        cost_estimate=pl.CostEstimate(flops=flops, bytes_accessed=moved, transcendentals=0),
        compiler_params=pltpu.CompilerParams(vmem_limit_bytes=limit),
    )(*args, *[one for one, _, _ in parts], *tokens)


def join_kernel(shape, places):
    def body(*refs):
        out = refs[-2]
        copies = [
            pltpu.make_async_copy(refs[i].at[source], out.at[target], refs[-1].at[n])
            for n, (i, source, target) in enumerate(places)
        ]
        for copy in copies:
            copy.start()
        for copy in copies:
            copy.wait()

    return body


def join(shape, places, *arrays, token=None):
    arrays = arrays if token is None else arrays + (token,)
    body = join_kernel(shape, places)

    def kernel(*refs):
        body(*refs[: len(arrays)], *refs[len(arrays) :])

    return pl.pallas_call(
        kernel,
        in_specs=[ANY] * len(arrays),
        out_specs=VMEM,
        out_shape=jax.ShapeDtypeStruct(shape, arrays[0].dtype),
        scratch_shapes=[pltpu.SemaphoreType.DMA((len(places),))],
        cost_estimate=pl.CostEstimate(flops=0, bytes_accessed=1 << 20, transcendentals=0),
        compiler_params=pltpu.CompilerParams(vmem_limit_bytes=SMALL),
    )(*arrays)


ALL, ONE, TWO = pl.ds(0, 256), pl.ds(0, 128), pl.ds(128, 128)


def both_of(held, bit):
    near, far = pl.ds(0, bit), pl.ds(bit, bit)
    return join(
        (2 * bit, 144, HEAD), [(0, near, near), (1, near, far)], held, to_replica(held, bit)
    )


def beyond(left, right, token=None):
    return (
        to_right(join((128, 512), [(0, ONE, ONE)], left, token=token)),
        to_left(join((128, 512), [(0, TWO, ONE)], right, token=token)),
    )


def along_x(own, right, far_a, far_b, left):
    places = [(0, ALL, (0, ALL)), (1, ALL, (1, ALL)), (4, ALL, (3, ALL))]
    places += [(2, ONE, (2, ONE)), (3, ONE, (2, TWO))]
    return join((4, 256, 512), places, own, right, far_a, far_b, left)


def stacked(pieces):
    return jnp.concatenate(pieces, axis=0)


def pack_gradients(a, b, c, d, out):
    refs = (a, b, c, d)
    for r in range(N):
        for j in range(0, 12, 2):
            out[r, 4 * j : 4 * j + 8] = stacked(
                [
                    refs[i][0, 4 * r : 4 * r + 4, at : at + HEAD]
                    for i, at in BLOCKS[j : j + 2]
                ]
            )


def pack_state(*refs):
    out = refs[-1]
    for q in range(3):
        rows = stacked([refs[4 * q + i][:, at : at + HEAD] for i, at in BLOCKS])
        out[0, 48 * q : 48 * q + 48] = rows.astype(bf16)


def sum_gradients(parts, summed, message):
    total = jnp.sum(parts[...], axis=0)
    for j, (i, at) in enumerate(BLOCKS):
        summed[:, j * HEAD : (j + 1) * HEAD] = total[4 * j : 4 * j + 4]
    squares = jnp.full((16, HEAD), jnp.sum(total * total))
    high = squares.astype(bf16).astype(f32)
    rows = lax.broadcasted_iota(jnp.int32, (16, HEAD), 0)
    tail = jnp.where(rows == 0, high, squares - high)
    whole = jnp.concatenate([total, tail], axis=0).astype(bf16)
    message[...] = jnp.broadcast_to(whole[None], message.shape)


def column_squares(parts, message):
    tails = parts[:, 48:64, 0:HEAD].astype(f32)
    rows = lax.broadcasted_iota(jnp.int32, tails.shape, 1)
    lanes = lax.broadcasted_iota(jnp.int32, tails.shape, 2)
    total = jnp.sum(jnp.where((rows < 2) & (lanes == 0), tails, 0.0))
    message[...] = jnp.full(message.shape, total)


def clip_of(squares):
    total = jnp.sum(jnp.max(squares[:, 0], axis=1, keepdims=True), axis=0, keepdims=True)
    return jnp.minimum(1.0, math.sqrt(PARAMS) / (jnp.sqrt(total) + norm_eps))


def make_copies(
    me, hidden, squares, parts, state_near, state_far, message, up, out_down, out_up, copies
):
    clip = clip_of(squares)
    for r in range(N):
        place = me[0] ^ r
        near, far = state_near[place & 7], state_far[place & 7]
        state = jnp.where(place < 8, near, far).astype(f32)
        new, _, _ = adam_update(
            state[0:48], parts[r, 0:48].astype(f32), state[48:96], state[96:144], clip
        )
        copies[r] = new

    def block(j):
        return stacked([copies[r, 4 * j : 4 * j + 4] for r in range(N)]).astype(bf16)

    blocks = [block(j) for j in range(12)]
    low = dot(hidden[...], jnp.concatenate(blocks[0:4], axis=1), ((1,), (1,)))
    low = jnp.concatenate([low[:128], low[128:]], axis=1).astype(bf16)
    message[...] = jnp.broadcast_to(low[None], message.shape)
    for target, first, last in ((up, 4, 6), (out_down, 6, 8), (out_up, 8, 12)):
        for j in range(first, last):
            target[:, (j - first) * HEAD : (j - first + 1) * HEAD] = blocks[j]


def update_state(*refs):
    squares, ins, summed, outs = refs[0], refs[1:13], refs[13], refs[14:]
    clip = clip_of(squares)
    at = 0
    for i, width in enumerate(WIDTHS):
        results = adam_update(
            ins[i][...], summed[:, at : at + width], ins[4 + i][...], ins[8 + i][...], clip
        )
        for q in range(3):
            outs[4 * q + i][...] = results[q]
        at += width


def base_queries(dz, order, weight, *refs):
    before = refs[0] if dz == 1 else None
    mine, other, out = refs[dz:]
    total = jnp.zeros((256, 256), f32)
    weight = weight.there()
    for dx in range(4):
        for flip, pieces in enumerate((mine, other)):
            place = order[2 * dx + dz] ^ flip
            total += dot(pieces[dx], weight[pl.ds(pl.multiple_of(place * 512, 512), 512), :])
    out[...] = total if before is None else total + before[...]


ROWS = 16


def attention(low, base, up, tables, cache, fresh, out):
    ups = up[...]
    zero = jnp.zeros_like(ups)
    lows = jnp.sum(low[...].astype(f32), axis=0).astype(bf16)
    turned = []
    for step in range(2):
        both = jnp.concatenate([ups, zero] if step == 0 else [zero, ups], axis=0)
        query = base[step * 128 : (step + 1) * 128] + 0.5 * dot(lows, both)
        for head in range(2):
            one = query[:, head * HEAD : (head + 1) * HEAD]
            one = one * tables[step] + pltpu.roll(one, HEAD // 2, 1) * tables[2 + step]
            turned.append((one * (1.0 / math.sqrt(HEAD))).astype(bf16))
    shape = (4 * ROWS, ROWS * 32)
    slots = lax.broadcasted_iota(jnp.int32, shape, 1)
    rows = lax.broadcasted_iota(jnp.int32, shape, 0) & (ROWS - 1)
    own = (slots >> 5) == rows
    slots = (slots & 31).astype(f32)
    new_shape = (4 * ROWS, ROWS * 2)
    new_slots = lax.broadcasted_iota(jnp.int32, new_shape, 1)
    new_index = lax.broadcasted_iota(jnp.int32, new_shape, 0)
    new_live = ((new_slots >> 1) == (new_index & (ROWS - 1))) & (
        (new_slots & 1) <= (new_index >> 5)
    )
    for k in range(128 // ROWS):
        at = k * ROWS
        queries = stacked([one[at : at + ROWS] for one in turned])
        held = cache[at * 32 : (at + ROWS) * 32]
        new = fresh[at * 2 : (at + ROWS) * 2]
        scores = dot(queries, held[:, :HEAD], ((1,), (1,)))
        new_scores = dot(queries, new[:, :HEAD], ((1,), (1,)))
        length = stacked([tables[4, at : at + ROWS]] * 4)
        length = jnp.concatenate([length] * (shape[1] // HEAD), axis=1)
        scores = jnp.where(own & (slots < length), scores, -1e30)
        new_scores = jnp.where(new_live, new_scores, -1e30)
        top = jnp.maximum(
            jnp.max(scores, axis=1, keepdims=True), jnp.max(new_scores, axis=1, keepdims=True)
        )
        weights = jnp.exp(scores - top)
        new_weights = jnp.exp(new_scores - top)
        total = jnp.sum(weights, axis=1, keepdims=True)
        total = total + jnp.sum(new_weights, axis=1, keepdims=True)
        inverse = 1.0 / total
        result = dot((weights * inverse).astype(bf16), held[:, HEAD:])
        result = result + dot((new_weights * inverse).astype(bf16), new[:, HEAD:])
        for step in range(2):
            for head in range(2):
                first = (step * 2 + head) * ROWS
                out[
                    step * 128 + at : step * 128 + at + ROWS, head * HEAD : (head + 1) * HEAD
                ] = result[first : first + ROWS].astype(bf16)


def give_columns(core, *refs):
    weight, out = refs[:8], refs[8]
    for k in range(8):
        out[:, k * 512 : (k + 1) * 512] = weight[k][...]


def columns(k, other):
    def view(ref, order):
        place = order[k] >> 1 if other else order[k]
        return ref.at[:, pl.ds(pl.multiple_of(place * 512, 512), 512)]

    return view


def columns_of(weights, k):
    return [(w, (256, 512), columns(k, i == 1)) for i, w in enumerate(weights)]


def lay_out(counts, order, *refs):
    total = sum(counts)
    blocks, outs = list(refs[: 2 * total]), refs[2 * total :]
    for out, count in zip(outs, counts):
        for i in range(count):
            out[i, :256] = blocks.pop(0)[...]
            out[i, 256:] = blocks.pop(0)[...]


def project_far(mine, other, weight, down, down_other, right, left, low):
    inner = dot(mine[...], down[...], ((1,), (1,))) + dot(
        other[...], down_other[...], ((1,), (1,))
    )
    packed = jnp.concatenate([inner[32 * i : 32 * i + 32] for i in range(8)], axis=1)
    low[...] = packed
    right[128:] = packed.astype(bf16)
    left[128:] = packed.astype(bf16)
    both = jnp.concatenate([mine[...], other[...]], axis=1)
    result = dot(both, weight[0])
    right[:128] = result[:128].astype(bf16)
    left[:128] = result[128:].astype(bf16)


def project_near(mine, other, weight, *targets):
    both = jnp.concatenate([mine[...], other[...]], axis=1)
    for i, target in enumerate(targets):
        target[...] = dot(both, weight[i])


def project_later(mine, other, weight, right, left, *targets):
    both = jnp.concatenate([mine[...], other[...]], axis=1)
    result = dot(both, weight[0])
    right[...] = result[:128].astype(bf16)
    left[...] = result[128:].astype(bf16)
    for i, target in enumerate(targets):
        target[...] = dot(both, weight[i + 1])


def forward(right, left, from_left, from_right, go_right, go_left):
    go_right[:128] = (right[:128] + from_left[:128].astype(f32)).astype(bf16)
    go_right[128:256] = right[128:].astype(bf16)
    go_left[:128] = left[:128].astype(bf16)
    go_left[128:256] = (left[128:] + from_right[:128].astype(f32)).astype(bf16)
    if go_right.shape[0] > 256:
        go_right[256:] = from_left[128:]
        go_left[256:] = from_right[128:]


def add_x(keep, low, from_left, from_right, far_left, far_right, message):
    message[:256] = (
        keep[...] + far_left[:256].astype(f32) + far_right[:256].astype(f32)
    ).astype(bf16)
    message[256:] = (
        low[...]
        + from_left[128:].astype(f32)
        + from_right[128:].astype(f32)
        + far_left[256:].astype(f32)
    ).astype(bf16)


def own_part(keep, far_left, far_right, hidden, out):
    out[...] = (
        hidden[...].astype(f32)
        + keep[...]
        + far_left[...].astype(f32)
        + far_right[...].astype(f32)
    )


def finish(own, message, from_z, out_up, out):
    packed = (message[256:].astype(f32) + from_z[256:].astype(f32)).astype(bf16)
    inner = stacked([packed[:, 64 * i : 64 * i + 64] for i in range(8)])
    out[...] = (
        own[...] + from_z[:256].astype(f32) + 0.5 * dot(inner, out_up[...])
    ).astype(bf16)


def on_device(
    hidden,
    query_base_weight,
    output_base_weight,
    cache,
    fresh,
    lengths,
    grad_query_down,
    grad_query_up,
    grad_output_down,
    grad_output_up,
    *state,
):
    rank = lax.axis_index("tp")
    core = rank % 2
    z_hi = (rank // 2) % 2
    x = rank // 4

    steps = jnp.arange(8, dtype=jnp.int32)
    order = ((x + steps // 2) % 4) * 4 + (z_hi ^ (steps % 2)) * 2 + core

    gradient = call(
        pack_gradients,
        [((N, 48, HEAD), f32)],
        fetch=(grad_query_down, grad_query_up, grad_output_down, grad_output_up),
    )
    parts = lax.all_to_all(gradient, "rep", 0, 0)

    hidden = hidden.reshape(256, 512)
    left = to_right(hidden)
    right = to_left(hidden)
    held = call(pack_state, [((1, 144, HEAD), bf16)], fetch=state)
    held = both_of(held, 1)
    held = both_of(held, 2)

    summed, message = call(
        sum_gradients,
        [((4, 1536), f32), ((N, 64, HEAD), bf16)],
        parts,
        tokens=(left, right, held),
        moved=CHAIN,
        limit=SMALL,
    )
    all_parts = lax.all_to_all(message, "rep", 0, 0)
    far_a, far_b = beyond(left, right)
    held = both_of(held, 4)

    squares_sent = call(
        column_squares,
        [((N, 8, HEAD), f32)],
        all_parts,
        moved=CHAIN,
        limit=SMALL,
    )
    squares = lax.all_to_all(squares_sent, "tp", 0, 0)
    zed = to_z(join((256, 512), [(0, ALL, ALL)], hidden, token=summed))
    held_far = to_replica(held, 8)
    set_h = along_x(hidden, right, far_a, far_b, left)
    set_h_other = to_core(set_h)

    def given(k):
        return lambda ref, core: ref.at[
            :, pl.ds(pl.multiple_of((2 * k + 1 - core[0]) * 512, 512), 512)
        ]

    give = call(
        give_columns,
        [((256, 4096), bf16)],
        core.reshape(1),
        scalars=1,
        fetch=[(output_base_weight, (256, 512), given(k)) for k in range(8)],
        moved=4 << 20,
    )
    weights = (output_base_weight, to_core(give))
    used = ((5,), (3, 7), (4, 1, 2, 6, 0))
    counts = tuple(map(len, used))
    w_far, w_near, w_later = call(
        functools.partial(lay_out, counts),
        [((count, 512, 512), bf16) for count in counts],
        order,
        scalars=1,
        fetch=[one for ks in used for k in ks for one in columns_of(weights, k)],
        moved=8 << 20,
    )

    message, up, out_down, out_up = call(
        make_copies,
        [((N, 128, HEAD), bf16), ((64, 256), bf16), ((64, 256), bf16), ((64, 512), bf16)],
        lax.axis_index("rep").reshape(1),
        scalars=1,
        fetch=(hidden,),
        take=(squares, all_parts, held, held_far),
        moved=CHAIN,
        room=[pltpu.VMEM((N, 48, HEAD), f32)],
    )
    lows = lax.all_to_all(message, "tp", 0, 0)
    out_down_other = to_core(out_down)
    updated = call(
        update_state,
        [((4, w), f32) for _ in range(3) for w in WIDTHS],
        squares,
        fetch=state,
        take=(summed,),
    )
    left_z = to_right(zed)
    right_z = to_left(zed)
    set_z = along_x(zed, right_z, *beyond(left_z, right_z), left_z)
    set_z_other = to_core(set_z)
    cost = dict(scalars=1, flops=256 * 8192 * 256, moved=4 << 20)
    base = call(
        functools.partial(base_queries, 0),
        [((256, 256), f32)],
        order,
        fetch=(query_base_weight,),
        take=(set_h, set_h_other),
        **cost,
    )
    base = call(
        functools.partial(base_queries, 1),
        [((256, 256), f32)],
        order,
        fetch=(query_base_weight,),
        take=(base, set_z, set_z_other),
        **cost,
    )

    frequency = jnp.power(rope_base, -2.0 * jnp.arange(64, dtype=f32) / HEAD)
    positions = (lengths[None, :] + jnp.arange(2, dtype=jnp.int32)[:, None]).astype(f32)
    angles = positions[:, :, None] * frequency
    cosine = jnp.cos(angles)
    sine = jnp.sin(angles)
    tables = jnp.concatenate(
        [
            jnp.concatenate([cosine, cosine], axis=2),
            jnp.concatenate([-sine, sine], axis=2),
            jnp.broadcast_to(lengths.astype(f32)[None, :, None], (1, 128, HEAD)),
        ]
    )
    attended = call(
        attention,
        [((256, 256), bf16)],
        lows,
        base,
        up,
        tables,
        cache.reshape(4096, 256),
        fresh.reshape(256, 256),
        tokens=(w_far,),
        limit=SMALL,
        flops=2 * 512 * 512 * 256,
        moved=4 << 20,
    )

    attended_other = to_core(attended)
    far_right, far_left, low = call(
        project_far,
        [((160, 512), bf16), ((160, 512), bf16), ((32, 512), f32)],
        attended,
        attended_other,
        w_far,
        out_down,
        out_down_other,
        limit=SMALL,
        flops=2 * 256 * 512 * 512,
        moved=1 << 20,
    )
    from_left = to_right(far_right)
    from_right = to_left(far_left)
    near_right, near_left = call(
        project_near,
        [((256, 512), f32)] * 2,
        attended,
        attended_other,
        w_near,
        limit=SMALL,
        flops=2 * 256 * 512 * 1024,
        moved=2 << 20,
    )
    later_right, later_left, keep, later_near_right, later_near_left, later_keep = call(
        project_later,
        [((128, 512), bf16)] * 2 + [((256, 512), f32)] * 4,
        attended,
        attended_other,
        w_later,
        limit=SMALL,
        flops=2 * 256 * 512 * 2560,
        moved=5 << 20,
    )
    later_from_left = to_right(later_right)
    later_from_right = to_left(later_left)
    go_right, go_left = call(
        forward,
        [((288, 512), bf16)] * 2,
        near_right,
        near_left,
        from_left,
        from_right,
        limit=SMALL,
    )
    got_left = to_right(go_right)
    got_right = to_left(go_left)
    later_go_right, later_go_left = call(
        forward,
        [((256, 512), bf16)] * 2,
        later_near_right,
        later_near_left,
        later_from_left,
        later_from_right,
        limit=SMALL,
    )
    later_got_left = to_right(later_go_right)
    later_got_right = to_left(later_go_left)
    message = call(
        add_x,
        [((288, 512), bf16)],
        keep,
        low,
        from_left,
        from_right,
        got_left,
        got_right,
        limit=SMALL,
    )
    from_z = to_z(message)
    own = call(
        own_part,
        [((256, 512), f32)],
        later_keep,
        later_got_left,
        later_got_right,
        fetch=(hidden,),
        limit=SMALL,
    )
    decoded = call(
        finish, [((256, 512), bf16)], own, message, from_z, take=(out_up,), limit=SMALL
    )
    return (decoded.reshape(2, 128, 512), *updated)


def solution(mesh):
    return jax.shard_map(
        on_device,
        mesh=mesh,
        in_specs=(
            P(None, "rep", "tp"),
            P(None, "tp"),
            P("tp", None),
            P("rep", "tp", None, None),
            P("rep", "tp", None, None),
            P("rep"),
        )
        + (P("rep", None, "tp"),) * 4
        + (P("rep", "tp"),) * 12,
        out_specs=(P(None, "rep", "tp"),) + (P("rep", "tp"),) * 12,
        check_vma=False,
    )
```

```python
import functools
import math

import jax
import jax.numpy as jnp
from jax import lax
from jax.experimental import pallas as pl
from jax.experimental.pallas import tpu as pltpu
from jax.sharding import PartitionSpec as P

HEAD = 128
PARAMS = 1572864
N = 16

beta_one = 0.9
beta_two = 0.999
bias_one = 1.0 - math.exp(1000.0 * math.log(0.9))
bias_two = 1.0 - math.exp(1000.0 * math.log(0.999))
adam_eps = 1e-08
learn_rate = 0.005
norm_eps = 1e-06
rope_base = 1000000.0

bf16 = jnp.bfloat16
f32 = jnp.float32


def adam_update(factor, gradient, moment, square, clip_factor):
    scaled = clip_factor * gradient
    moment_new = beta_one * moment + (1.0 - beta_one) * scaled
    square_new = beta_two * square + (1.0 - beta_two) * scaled * scaled
    update = moment_new / bias_one / (jnp.sqrt(square_new / bias_two) + adam_eps)
    return (factor - learn_rate * update, moment_new, square_new)


def shift(value, move):
    return lax.ppermute(value, "tp", [(i, move(i)) for i in range(N)])


def to_core(value):
    return shift(value, lambda i: i ^ 1)


def to_z(value):
    return shift(value, lambda i: i ^ 2)


def to_replica(value, bit):
    return lax.ppermute(value, "rep", [(i, i ^ bit) for i in range(N)])


def to_right(value):
    return shift(value, lambda i: (i + 4) % N)


def to_across(value):
    return shift(value, lambda i: (i + 8) % N)


def to_left(value):
    return shift(value, lambda i: (i + 12) % N)


def dot(a, b, contract=((1,), (0,))):
    return lax.dot_general(a, b, (contract, ((), ())), preferred_element_type=f32)


VMEM = pl.BlockSpec(memory_space=pltpu.VMEM)
SMEM = pl.BlockSpec(memory_space=pltpu.SMEM)
ANY = pl.BlockSpec(memory_space=pl.ANY)
HBM = pl.BlockSpec(memory_space=pltpu.HBM)
LARGE, SMALL = 60 << 20, 24 << 20
CHAIN = 48 << 20
WIDTHS = (512, 256, 256, 512)
BLOCKS = [(i, c) for i, w in enumerate(WIDTHS) for c in range(0, w, HEAD)]


class Fetched:
    def __init__(self, copy, ref):
        self.copy, self.ref, self.waited = copy, ref, False

    def there(self):
        if not self.waited:
            self.copy.wait()
            self.waited = True
        return self.ref

    def __getitem__(self, index):
        return self.there()[index]


def call(kernel, shapes, *args, scalars=0, fetch=(), take=(), tokens=(), room=(), limit=LARGE, flops=0, moved=1 << 20):
    out = [jax.ShapeDtypeStruct(s, d) for s, d in shapes]
    single = len(out) == 1
    parts = [f if isinstance(f, tuple) else (f, f.shape, None) for f in (*fetch, *take)]
    first, count = len(args), len(args) + len(parts)
    skip = count + len(tokens)

    def body(*refs):
        ins, outs = refs[:count], refs[skip : skip + len(out)]
        scratch = refs[skip + len(out) :]
        held = []
        for i, (_, _, view) in enumerate(parts):
            source = ins[first + i]
            if view is not None:
                source = view(source, *ins[:scalars])
            copy = pltpu.make_async_copy(source, scratch[i], scratch[len(parts)].at[i])
            copy.start()
            held.append(Fetched(copy, scratch[i]))
        kernel(*ins[:first], *held, *outs, *scratch[len(scratch) - len(room) :])
        for one in held:
            one.there()

    return pl.pallas_call(
        body,
        in_specs=[SMEM] * scalars
        + [VMEM] * (first - scalars)
        + [HBM] * len(fetch)
        + [ANY] * (len(take) + len(tokens)),
        out_specs=VMEM if single else [VMEM] * len(out),
        out_shape=out[0] if single else out,
        scratch_shapes=[pltpu.VMEM(shape, one.dtype) for one, shape, _ in parts]
        + ([pltpu.SemaphoreType.DMA((len(parts),))] if parts else [])
        + list(room),
        cost_estimate=pl.CostEstimate(flops=flops, bytes_accessed=moved, transcendentals=0),
        compiler_params=pltpu.CompilerParams(vmem_limit_bytes=limit),
    )(*args, *[one for one, _, _ in parts], *tokens)


def join_kernel(shape, places):
    def body(*refs):
        out = refs[-2]
        copies = [
            pltpu.make_async_copy(refs[i].at[source], out.at[target], refs[-1].at[n])
            for n, (i, source, target) in enumerate(places)
        ]
        for copy in copies:
            copy.start()
        for copy in copies:
            copy.wait()

    return body


def join(shape, places, *arrays, token=None):
    arrays = arrays if token is None else arrays + (token,)
    body = join_kernel(shape, places)

    def kernel(*refs):
        body(*refs[: len(arrays)], *refs[len(arrays) :])

    return pl.pallas_call(
        kernel,
        in_specs=[ANY] * len(arrays),
        out_specs=VMEM,
        out_shape=jax.ShapeDtypeStruct(shape, arrays[0].dtype),
        scratch_shapes=[pltpu.SemaphoreType.DMA((len(places),))],
        cost_estimate=pl.CostEstimate(flops=0, bytes_accessed=1 << 20, transcendentals=0),
        compiler_params=pltpu.CompilerParams(vmem_limit_bytes=SMALL),
    )(*arrays)


ALL = pl.ds(0, 256)


def both_of(held, bit):
    near, far = pl.ds(0, bit), pl.ds(bit, bit)
    return join(
        (2 * bit, 144, HEAD), [(0, near, near), (1, near, far)], held, to_replica(held, bit)
    )


def along_x(*pieces):
    places = [(dx, ALL, (dx, ALL)) for dx in range(4)]
    return join((4, 256, 512), places, *pieces)


def stacked(pieces):
    return jnp.concatenate(pieces, axis=0)


def pack_gradients(a, b, c, d, out):
    refs = (a, b, c, d)
    for r in range(N):
        for j in range(0, 12, 2):
            out[r, 4 * j : 4 * j + 8] = stacked(
                [
                    refs[i][0, 4 * r : 4 * r + 4, at : at + HEAD]
                    for i, at in BLOCKS[j : j + 2]
                ]
            )


def pack_state(*refs):
    out = refs[-1]
    for q in range(3):
        rows = stacked([refs[4 * q + i][:, at : at + HEAD] for i, at in BLOCKS])
        out[0, 48 * q : 48 * q + 48] = rows.astype(bf16)


def sum_gradients(parts, summed, message):
    total = jnp.sum(parts[...], axis=0)
    for j, (i, at) in enumerate(BLOCKS):
        summed[:, j * HEAD : (j + 1) * HEAD] = total[4 * j : 4 * j + 4]
    squares = jnp.full((16, HEAD), jnp.sum(total * total))
    high = squares.astype(bf16).astype(f32)
    rows = lax.broadcasted_iota(jnp.int32, (16, HEAD), 0)
    tail = jnp.where(rows == 0, high, squares - high)
    whole = jnp.concatenate([total, tail], axis=0).astype(bf16)
    message[...] = jnp.broadcast_to(whole[None], message.shape)


def column_squares(parts, message):
    tails = parts[:, 48:64, 0:HEAD].astype(f32)
    rows = lax.broadcasted_iota(jnp.int32, tails.shape, 1)
    lanes = lax.broadcasted_iota(jnp.int32, tails.shape, 2)
    total = jnp.sum(jnp.where((rows < 2) & (lanes == 0), tails, 0.0))
    message[...] = jnp.full(message.shape, total)


def clip_of(squares):
    total = jnp.sum(jnp.max(squares[:, 0], axis=1, keepdims=True), axis=0, keepdims=True)
    return jnp.minimum(1.0, math.sqrt(PARAMS) / (jnp.sqrt(total) + norm_eps))


def make_copies(
    me, hidden, squares, parts, state_near, state_far, message, up, out_down, out_up, copies
):
    clip = clip_of(squares)
    for r in range(N):
        place = me[0] ^ r
        near, far = state_near[place & 7], state_far[place & 7]
        state = jnp.where(place < 8, near, far).astype(f32)
        new, _, _ = adam_update(
            state[0:48], parts[r, 0:48].astype(f32), state[48:96], state[96:144], clip
        )
        copies[r] = new

    def block(j):
        return stacked([copies[r, 4 * j : 4 * j + 4] for r in range(N)]).astype(bf16)

    blocks = [block(j) for j in range(12)]
    low = dot(hidden[...], jnp.concatenate(blocks[0:4], axis=1), ((1,), (1,)))
    low = jnp.concatenate([low[:128], low[128:]], axis=1).astype(bf16)
    message[...] = jnp.broadcast_to(low[None], message.shape)
    for target, first, last in ((up, 4, 6), (out_down, 6, 8), (out_up, 8, 12)):
        for j in range(first, last):
            target[:, (j - first) * HEAD : (j - first + 1) * HEAD] = blocks[j]


def update_state(*refs):
    squares, ins, summed, outs = refs[0], refs[1:13], refs[13], refs[14:]
    clip = clip_of(squares)
    at = 0
    for i, width in enumerate(WIDTHS):
        results = adam_update(
            ins[i][...], summed[:, at : at + width], ins[4 + i][...], ins[8 + i][...], clip
        )
        for q in range(3):
            outs[4 * q + i][...] = results[q]
        at += width


def base_queries(order, weight, *refs):
    sets, out = refs[:4], refs[4]
    total = jnp.zeros((256, 256), f32)
    for i, pieces in enumerate(sets):
        for dx in range(4):
            place = order[2 * dx + i // 2] ^ (i % 2)
            rows = pl.ds(pl.multiple_of(place * 512, 512), 512)
            total += dot(pieces[dx], weight[rows, :])
    out[...] = total


ROWS = 16


def attention(low, base, up, tables, cache, fresh, out):
    ups = up[...]
    zero = jnp.zeros_like(ups)
    lows = jnp.sum(low[...].astype(f32), axis=0).astype(bf16)
    turned = []
    for step in range(2):
        both = jnp.concatenate([ups, zero] if step == 0 else [zero, ups], axis=0)
        query = base[step * 128 : (step + 1) * 128] + 0.5 * dot(lows, both)
        for head in range(2):
            one = query[:, head * HEAD : (head + 1) * HEAD]
            one = one * tables[step] + pltpu.roll(one, HEAD // 2, 1) * tables[2 + step]
            turned.append((one * (1.0 / math.sqrt(HEAD))).astype(bf16))
    shape = (4 * ROWS, ROWS * 32)
    slots = lax.broadcasted_iota(jnp.int32, shape, 1)
    rows = lax.broadcasted_iota(jnp.int32, shape, 0) & (ROWS - 1)
    own = (slots >> 5) == rows
    slots = (slots & 31).astype(f32)
    new_shape = (4 * ROWS, ROWS * 2)
    new_slots = lax.broadcasted_iota(jnp.int32, new_shape, 1)
    new_index = lax.broadcasted_iota(jnp.int32, new_shape, 0)
    new_live = ((new_slots >> 1) == (new_index & (ROWS - 1))) & (
        (new_slots & 1) <= (new_index >> 5)
    )
    for k in range(128 // ROWS):
        at = k * ROWS
        queries = stacked([one[at : at + ROWS] for one in turned])
        held = cache[at * 32 : (at + ROWS) * 32]
        new = fresh[at * 2 : (at + ROWS) * 2]
        scores = dot(queries, held[:, :HEAD], ((1,), (1,)))
        new_scores = dot(queries, new[:, :HEAD], ((1,), (1,)))
        length = stacked([tables[4, at : at + ROWS]] * 4)
        length = jnp.concatenate([length] * (shape[1] // HEAD), axis=1)
        scores = jnp.where(own & (slots < length), scores, -1e30)
        new_scores = jnp.where(new_live, new_scores, -1e30)
        top = jnp.maximum(
            jnp.max(scores, axis=1, keepdims=True), jnp.max(new_scores, axis=1, keepdims=True)
        )
        weights = jnp.exp(scores - top)
        new_weights = jnp.exp(new_scores - top)
        total = jnp.sum(weights, axis=1, keepdims=True)
        total = total + jnp.sum(new_weights, axis=1, keepdims=True)
        inverse = 1.0 / total
        result = dot((weights * inverse).astype(bf16), held[:, HEAD:])
        result = result + dot((new_weights * inverse).astype(bf16), new[:, HEAD:])
        for step in range(2):
            for head in range(2):
                first = (step * 2 + head) * ROWS
                out[
                    step * 128 + at : step * 128 + at + ROWS, head * HEAD : (head + 1) * HEAD
                ] = result[first : first + ROWS].astype(bf16)


def give_columns(core, *refs):
    weight, out = refs[:8], refs[8]
    for k in range(8):
        out[:, k * 512 : (k + 1) * 512] = weight[k][...]


def columns(k, other):
    def view(ref, order):
        place = order[k] >> 1 if other else order[k]
        return ref.at[:, pl.ds(pl.multiple_of(place * 512, 512), 512)]

    return view


def columns_of(weights, k):
    return [(w, (256, 512), columns(k, i == 1)) for i, w in enumerate(weights)]


def lay_out(counts, order, *refs):
    total = sum(counts)
    blocks, outs = list(refs[: 2 * total]), refs[2 * total :]
    for out, count in zip(outs, counts):
        for i in range(count):
            out[i, :256] = blocks.pop(0)[...]
            out[i, 256:] = blocks.pop(0)[...]


def project_far(mine, other, weight, down, down_other, right, left, low):
    inner = dot(mine[...], down[...], ((1,), (1,))) + dot(
        other[...], down_other[...], ((1,), (1,))
    )
    packed = jnp.concatenate([inner[32 * i : 32 * i + 32] for i in range(8)], axis=1)
    low[...] = packed
    right[128:] = packed.astype(bf16)
    left[128:] = packed.astype(bf16)
    both = jnp.concatenate([mine[...], other[...]], axis=1)
    result = dot(both, weight[0])
    right[:128] = result[:128].astype(bf16)
    left[:128] = result[128:].astype(bf16)


def project_near(mine, other, weight, *targets):
    both = jnp.concatenate([mine[...], other[...]], axis=1)
    for i, target in enumerate(targets):
        target[...] = dot(both, weight[i])


def project_later(mine, other, weight, right, left, *targets):
    both = jnp.concatenate([mine[...], other[...]], axis=1)
    result = dot(both, weight[0])
    right[...] = result[:128].astype(bf16)
    left[...] = result[128:].astype(bf16)
    for i, target in enumerate(targets):
        target[...] = dot(both, weight[i + 1])


def forward(right, left, from_left, from_right, go_right, go_left):
    go_right[:128] = (right[:128] + from_left[:128].astype(f32)).astype(bf16)
    go_right[128:256] = right[128:].astype(bf16)
    go_left[:128] = left[:128].astype(bf16)
    go_left[128:256] = (left[128:] + from_right[:128].astype(f32)).astype(bf16)
    if go_right.shape[0] > 256:
        go_right[256:] = from_left[128:]
        go_left[256:] = from_right[128:]


def add_x(keep, low, from_left, from_right, far_left, far_right, message):
    message[:256] = (
        keep[...] + far_left[:256].astype(f32) + far_right[:256].astype(f32)
    ).astype(bf16)
    message[256:] = (
        low[...]
        + from_left[128:].astype(f32)
        + from_right[128:].astype(f32)
        + far_left[256:].astype(f32)
    ).astype(bf16)


def own_part(keep, far_left, far_right, hidden, out):
    out[...] = (
        hidden[...].astype(f32)
        + keep[...]
        + far_left[...].astype(f32)
        + far_right[...].astype(f32)
    )


def finish(own, message, from_z, out_up, out):
    packed = (message[256:].astype(f32) + from_z[256:].astype(f32)).astype(bf16)
    inner = stacked([packed[:, 64 * i : 64 * i + 64] for i in range(8)])
    out[...] = (
        own[...] + from_z[:256].astype(f32) + 0.5 * dot(inner, out_up[...])
    ).astype(bf16)


def on_device(
    hidden,
    query_base_weight,
    output_base_weight,
    cache,
    fresh,
    lengths,
    grad_query_down,
    grad_query_up,
    grad_output_down,
    grad_output_up,
    *state,
):
    rank = lax.axis_index("tp")
    core = rank % 2
    z_hi = (rank // 2) % 2
    x = rank // 4

    steps = jnp.arange(8, dtype=jnp.int32)
    order = ((x + steps // 2) % 4) * 4 + (z_hi ^ (steps % 2)) * 2 + core

    gradient = call(
        pack_gradients,
        [((N, 48, HEAD), f32)],
        fetch=(grad_query_down, grad_query_up, grad_output_down, grad_output_up),
    )
    parts = lax.all_to_all(gradient, "rep", 0, 0)

    hidden = hidden.reshape(256, 512)
    left = to_right(hidden)
    right = to_left(hidden)
    across = to_across(hidden)
    held = call(pack_state, [((1, 144, HEAD), bf16)], fetch=state)
    held = both_of(held, 1)
    held = both_of(held, 2)

    summed, message = call(
        sum_gradients,
        [((4, 1536), f32), ((N, 64, HEAD), bf16)],
        parts,
        tokens=(left, right, across, held),
        moved=CHAIN,
        limit=SMALL,
    )
    all_parts = lax.all_to_all(message, "rep", 0, 0)
    held = both_of(held, 4)

    squares_sent = call(
        column_squares,
        [((N, 8, HEAD), f32)],
        all_parts,
        moved=CHAIN,
        limit=SMALL,
    )
    squares = lax.all_to_all(squares_sent, "tp", 0, 0)
    zed = to_z(join((256, 512), [(0, ALL, ALL)], hidden, token=summed))
    held_far = to_replica(held, 8)
    set_h = along_x(hidden, right, across, left)
    set_h_other = to_core(set_h)

    def given(k):
        return lambda ref, core: ref.at[
            :, pl.ds(pl.multiple_of((2 * k + 1 - core[0]) * 512, 512), 512)
        ]

    give = call(
        give_columns,
        [((256, 4096), bf16)],
        core.reshape(1),
        scalars=1,
        fetch=[(output_base_weight, (256, 512), given(k)) for k in range(8)],
        moved=4 << 20,
    )
    weights = (output_base_weight, to_core(give))
    used = ((5,), (3, 7), (4, 1, 2, 6, 0))
    counts = tuple(map(len, used))
    w_far, w_near, w_later = call(
        functools.partial(lay_out, counts),
        [((count, 512, 512), bf16) for count in counts],
        order,
        scalars=1,
        fetch=[one for ks in used for k in ks for one in columns_of(weights, k)],
        moved=8 << 20,
    )

    message, up, out_down, out_up = call(
        make_copies,
        [((N, 128, HEAD), bf16), ((64, 256), bf16), ((64, 256), bf16), ((64, 512), bf16)],
        lax.axis_index("rep").reshape(1),
        scalars=1,
        fetch=(hidden,),
        take=(squares, all_parts, held, held_far),
        moved=CHAIN,
        room=[pltpu.VMEM((N, 48, HEAD), f32)],
    )
    lows = lax.all_to_all(message, "tp", 0, 0)
    out_down_other = to_core(out_down)
    updated = call(
        update_state,
        [((4, w), f32) for _ in range(3) for w in WIDTHS],
        squares,
        fetch=state,
        take=(summed,),
    )
    set_z = along_x(zed, to_left(zed), to_across(zed), to_right(zed))
    set_z_other = to_core(set_z)
    base = call(
        base_queries,
        [((256, 256), f32)],
        order,
        scalars=1,
        fetch=(query_base_weight,),
        take=(set_h, set_h_other, set_z, set_z_other),
        flops=2 * 256 * 8192 * 256,
        moved=8 << 20,
    )

    frequency = jnp.power(rope_base, -2.0 * jnp.arange(64, dtype=f32) / HEAD)
    positions = (lengths[None, :] + jnp.arange(2, dtype=jnp.int32)[:, None]).astype(f32)
    angles = positions[:, :, None] * frequency
    cosine = jnp.cos(angles)
    sine = jnp.sin(angles)
    tables = jnp.concatenate(
        [
            jnp.concatenate([cosine, cosine], axis=2),
            jnp.concatenate([-sine, sine], axis=2),
            jnp.broadcast_to(lengths.astype(f32)[None, :, None], (1, 128, HEAD)),
        ]
    )
    attended = call(
        attention,
        [((256, 256), bf16)],
        lows,
        base,
        up,
        tables,
        cache.reshape(4096, 256),
        fresh.reshape(256, 256),
        tokens=(w_far,),
        limit=SMALL,
        flops=2 * 512 * 512 * 256,
        moved=4 << 20,
    )

    attended_other = to_core(attended)
    far_right, far_left, low = call(
        project_far,
        [((160, 512), bf16), ((160, 512), bf16), ((32, 512), f32)],
        attended,
        attended_other,
        w_far,
        out_down,
        out_down_other,
        limit=SMALL,
        flops=2 * 256 * 512 * 512,
        moved=1 << 20,
    )
    from_left = to_right(far_right)
    from_right = to_left(far_left)
    near_right, near_left = call(
        project_near,
        [((256, 512), f32)] * 2,
        attended,
        attended_other,
        w_near,
        limit=SMALL,
        flops=2 * 256 * 512 * 1024,
        moved=2 << 20,
    )
    later_right, later_left, keep, later_near_right, later_near_left, later_keep = call(
        project_later,
        [((128, 512), bf16)] * 2 + [((256, 512), f32)] * 4,
        attended,
        attended_other,
        w_later,
        limit=SMALL,
        flops=2 * 256 * 512 * 2560,
        moved=5 << 20,
    )
    later_from_left = to_right(later_right)
    later_from_right = to_left(later_left)
    go_right, go_left = call(
        forward,
        [((288, 512), bf16)] * 2,
        near_right,
        near_left,
        from_left,
        from_right,
        limit=SMALL,
    )
    got_left = to_right(go_right)
    got_right = to_left(go_left)
    later_go_right, later_go_left = call(
        forward,
        [((256, 512), bf16)] * 2,
        later_near_right,
        later_near_left,
        later_from_left,
        later_from_right,
        limit=SMALL,
    )
    later_got_left = to_right(later_go_right)
    later_got_right = to_left(later_go_left)
    message = call(
        add_x,
        [((288, 512), bf16)],
        keep,
        low,
        from_left,
        from_right,
        got_left,
        got_right,
        limit=SMALL,
    )
    from_z = to_z(message)
    own = call(
        own_part,
        [((256, 512), f32)],
        later_keep,
        later_got_left,
        later_got_right,
        fetch=(hidden,),
        limit=SMALL,
    )
    decoded = call(
        finish, [((256, 512), bf16)], own, message, from_z, take=(out_up,), limit=SMALL
    )
    return (decoded.reshape(2, 128, 512), *updated)


def solution(mesh):
    return jax.shard_map(
        on_device,
        mesh=mesh,
        in_specs=(
            P(None, "rep", "tp"),
            P(None, "tp"),
            P("tp", None),
            P("rep", "tp", None, None),
            P("rep", "tp", None, None),
            P("rep"),
        )
        + (P("rep", None, "tp"),) * 4
        + (P("rep", "tp"),) * 12,
        out_specs=(P(None, "rep", "tp"),) + (P("rep", "tp"),) * 12,
        check_vma=False,
    )
```

```python
import functools
import math

import jax
import jax.numpy as jnp
from jax import lax
from jax.experimental import pallas as pl
from jax.experimental.pallas import tpu as pltpu
from jax.sharding import PartitionSpec as P

HEAD = 128
PARAMS = 1572864
N = 16

beta_one = 0.9
beta_two = 0.999
bias_one = 1.0 - math.exp(1000.0 * math.log(0.9))
bias_two = 1.0 - math.exp(1000.0 * math.log(0.999))
adam_eps = 1e-08
learn_rate = 0.005
norm_eps = 1e-06
rope_base = 1000000.0

bf16 = jnp.bfloat16
f32 = jnp.float32


def adam_update(factor, gradient, moment, square, clip_factor):
    scaled = clip_factor * gradient
    moment_new = beta_one * moment + (1.0 - beta_one) * scaled
    square_new = beta_two * square + (1.0 - beta_two) * scaled * scaled
    update = moment_new / bias_one / (jnp.sqrt(square_new / bias_two) + adam_eps)
    return (factor - learn_rate * update, moment_new, square_new)


def shift(value, move):
    return lax.ppermute(value, "tp", [(i, move(i)) for i in range(N)])


def to_core(value):
    return shift(value, lambda i: i ^ 1)


def to_z(value):
    return shift(value, lambda i: i ^ 2)


def to_replica(value, bit):
    return lax.ppermute(value, "rep", [(i, i ^ bit) for i in range(N)])


def to_right(value):
    return shift(value, lambda i: (i + 4) % N)


def to_across(value):
    return shift(value, lambda i: (i + 8) % N)


def to_left(value):
    return shift(value, lambda i: (i + 12) % N)


def dot(a, b, contract=((1,), (0,))):
    return lax.dot_general(a, b, (contract, ((), ())), preferred_element_type=f32)


VMEM = pl.BlockSpec(memory_space=pltpu.VMEM)
SMEM = pl.BlockSpec(memory_space=pltpu.SMEM)
ANY = pl.BlockSpec(memory_space=pl.ANY)
HBM = pl.BlockSpec(memory_space=pltpu.HBM)
LARGE, SMALL = 60 << 20, 24 << 20
CHAIN = 48 << 20
WIDTHS = (512, 256, 256, 512)
BLOCKS = [(i, c) for i, w in enumerate(WIDTHS) for c in range(0, w, HEAD)]


class Fetched:
    def __init__(self, copy, ref):
        self.copy, self.ref, self.waited = copy, ref, False

    def there(self):
        if not self.waited:
            self.copy.wait()
            self.waited = True
        return self.ref

    def __getitem__(self, index):
        return self.there()[index]


def call(kernel, shapes, *args, scalars=0, fetch=(), take=(), tokens=(), room=(), limit=LARGE, flops=0, moved=1 << 20):
    out = [jax.ShapeDtypeStruct(s, d) for s, d in shapes]
    single = len(out) == 1
    parts = [f if isinstance(f, tuple) else (f, f.shape, None) for f in (*fetch, *take)]
    first, count = len(args), len(args) + len(parts)
    skip = count + len(tokens)

    def body(*refs):
        ins, outs = refs[:count], refs[skip : skip + len(out)]
        scratch = refs[skip + len(out) :]
        held = []
        for i, (_, _, view) in enumerate(parts):
            source = ins[first + i]
            if view is not None:
                source = view(source, *ins[:scalars])
            copy = pltpu.make_async_copy(source, scratch[i], scratch[len(parts)].at[i])
            copy.start()
            held.append(Fetched(copy, scratch[i]))
        kernel(*ins[:first], *held, *outs, *scratch[len(scratch) - len(room) :])
        for one in held:
            one.there()

    return pl.pallas_call(
        body,
        in_specs=[SMEM] * scalars
        + [VMEM] * (first - scalars)
        + [HBM] * len(fetch)
        + [ANY] * (len(take) + len(tokens)),
        out_specs=VMEM if single else [VMEM] * len(out),
        out_shape=out[0] if single else out,
        scratch_shapes=[pltpu.VMEM(shape, one.dtype) for one, shape, _ in parts]
        + ([pltpu.SemaphoreType.DMA((len(parts),))] if parts else [])
        + list(room),
        cost_estimate=pl.CostEstimate(flops=flops, bytes_accessed=moved, transcendentals=0),
        compiler_params=pltpu.CompilerParams(vmem_limit_bytes=limit),
    )(*args, *[one for one, _, _ in parts], *tokens)


def join_kernel(shape, places):
    def body(*refs):
        out = refs[-2]
        copies = [
            pltpu.make_async_copy(refs[i].at[source], out.at[target], refs[-1].at[n])
            for n, (i, source, target) in enumerate(places)
        ]
        for copy in copies:
            copy.start()
        for copy in copies:
            copy.wait()

    return body


def join(shape, places, *arrays, token=None):
    arrays = arrays if token is None else arrays + (token,)
    body = join_kernel(shape, places)

    def kernel(*refs):
        body(*refs[: len(arrays)], *refs[len(arrays) :])

    return pl.pallas_call(
        kernel,
        in_specs=[ANY] * len(arrays),
        out_specs=VMEM,
        out_shape=jax.ShapeDtypeStruct(shape, arrays[0].dtype),
        scratch_shapes=[pltpu.SemaphoreType.DMA((len(places),))],
        cost_estimate=pl.CostEstimate(flops=0, bytes_accessed=1 << 20, transcendentals=0),
        compiler_params=pltpu.CompilerParams(vmem_limit_bytes=SMALL),
    )(*arrays)


ALL = pl.ds(0, 256)


def both_of(held, bit):
    near, far = pl.ds(0, bit), pl.ds(bit, bit)
    return join(
        (2 * bit, 144, HEAD), [(0, near, near), (1, near, far)], held, to_replica(held, bit)
    )


def along_x(*pieces):
    places = [(dx, ALL, (dx, ALL)) for dx in range(4)]
    return join((4, 256, 512), places, *pieces)


def stacked(pieces):
    return jnp.concatenate(pieces, axis=0)


def pack_gradients(a, b, c, d, out):
    refs = (a, b, c, d)
    for r in range(N):
        for j in range(0, 12, 2):
            out[r, 4 * j : 4 * j + 8] = stacked(
                [
                    refs[i][0, 4 * r : 4 * r + 4, at : at + HEAD]
                    for i, at in BLOCKS[j : j + 2]
                ]
            )


def pack_state(*refs):
    out = refs[-1]
    for q in range(3):
        rows = stacked([refs[4 * q + i][:, at : at + HEAD] for i, at in BLOCKS])
        out[0, 48 * q : 48 * q + 48] = rows.astype(bf16)


def sum_gradients(parts, summed, message):
    total = jnp.sum(parts[...], axis=0)
    for j, (i, at) in enumerate(BLOCKS):
        summed[:, j * HEAD : (j + 1) * HEAD] = total[4 * j : 4 * j + 4]
    squares = jnp.full((16, HEAD), jnp.sum(total * total))
    high = squares.astype(bf16).astype(f32)
    rows = lax.broadcasted_iota(jnp.int32, (16, HEAD), 0)
    tail = jnp.where(rows == 0, high, squares - high)
    whole = jnp.concatenate([total, tail], axis=0).astype(bf16)
    message[...] = jnp.broadcast_to(whole[None], message.shape)


def column_squares(parts, message):
    tails = parts[:, 48:64, 0:HEAD].astype(f32)
    rows = lax.broadcasted_iota(jnp.int32, tails.shape, 1)
    lanes = lax.broadcasted_iota(jnp.int32, tails.shape, 2)
    total = jnp.sum(jnp.where((rows < 2) & (lanes == 0), tails, 0.0))
    message[...] = jnp.full(message.shape, total)


def clip_of(squares):
    total = jnp.sum(jnp.max(squares[:, 0], axis=1, keepdims=True), axis=0, keepdims=True)
    return jnp.minimum(1.0, math.sqrt(PARAMS) / (jnp.sqrt(total) + norm_eps))


def make_copies(
    me, hidden, squares, parts, state_near, state_far, message, up, out_down, out_up, copies
):
    clip = clip_of(squares)
    for r in range(N):
        place = me[0] ^ r
        near, far = state_near[place & 7], state_far[place & 7]
        state = jnp.where(place < 8, near, far).astype(f32)
        new, _, _ = adam_update(
            state[0:48], parts[r, 0:48].astype(f32), state[48:96], state[96:144], clip
        )
        copies[r] = new

    def block(j):
        return stacked([copies[r, 4 * j : 4 * j + 4] for r in range(N)]).astype(bf16)

    blocks = [block(j) for j in range(12)]
    low = dot(hidden[...], jnp.concatenate(blocks[0:4], axis=1), ((1,), (1,)))
    low = jnp.concatenate([low[:128], low[128:]], axis=1).astype(bf16)
    message[...] = jnp.broadcast_to(low[None], message.shape)
    for target, first, last in ((up, 4, 6), (out_down, 6, 8), (out_up, 8, 12)):
        for j in range(first, last):
            target[:, (j - first) * HEAD : (j - first + 1) * HEAD] = blocks[j]


def update_state(*refs):
    squares, ins, summed, outs = refs[0], refs[1:13], refs[13], refs[14:]
    clip = clip_of(squares)
    at = 0
    for i, width in enumerate(WIDTHS):
        results = adam_update(
            ins[i][...], summed[:, at : at + width], ins[4 + i][...], ins[8 + i][...], clip
        )
        for q in range(3):
            outs[4 * q + i][...] = results[q]
        at += width


def base_queries(order, weight, *refs):
    sets, out = refs[:4], refs[4]
    total = jnp.zeros((256, 256), f32)
    for i, pieces in enumerate(sets):
        for dx in range(4):
            place = order[2 * dx + i // 2] ^ (i % 2)
            rows = pl.ds(pl.multiple_of(place * 512, 512), 512)
            total += dot(pieces[dx], weight[rows, :])
    out[...] = total


ROWS = 16


def attention(low, base, up, tables, cache, fresh, out):
    ups = up[...]
    zero = jnp.zeros_like(ups)
    lows = jnp.sum(low[...].astype(f32), axis=0).astype(bf16)
    turned = []
    for step in range(2):
        both = jnp.concatenate([ups, zero] if step == 0 else [zero, ups], axis=0)
        query = base[step * 128 : (step + 1) * 128] + 0.5 * dot(lows, both)
        for head in range(2):
            one = query[:, head * HEAD : (head + 1) * HEAD]
            one = one * tables[step] + pltpu.roll(one, HEAD // 2, 1) * tables[2 + step]
            turned.append((one * (1.0 / math.sqrt(HEAD))).astype(bf16))
    shape = (4 * ROWS, ROWS * 32)
    slots = lax.broadcasted_iota(jnp.int32, shape, 1)
    rows = lax.broadcasted_iota(jnp.int32, shape, 0) & (ROWS - 1)
    own = (slots >> 5) == rows
    slots = (slots & 31).astype(f32)
    new_shape = (4 * ROWS, ROWS * 2)
    new_slots = lax.broadcasted_iota(jnp.int32, new_shape, 1)
    new_index = lax.broadcasted_iota(jnp.int32, new_shape, 0)
    new_live = ((new_slots >> 1) == (new_index & (ROWS - 1))) & (
        (new_slots & 1) <= (new_index >> 5)
    )
    for k in range(128 // ROWS):
        at = k * ROWS
        queries = stacked([one[at : at + ROWS] for one in turned])
        held = cache[at * 32 : (at + ROWS) * 32]
        new = fresh[at * 2 : (at + ROWS) * 2]
        scores = dot(queries, held[:, :HEAD], ((1,), (1,)))
        new_scores = dot(queries, new[:, :HEAD], ((1,), (1,)))
        length = stacked([tables[4, at : at + ROWS]] * 4)
        length = jnp.concatenate([length] * (shape[1] // HEAD), axis=1)
        scores = jnp.where(own & (slots < length), scores, -1e30)
        new_scores = jnp.where(new_live, new_scores, -1e30)
        top = jnp.maximum(
            jnp.max(scores, axis=1, keepdims=True), jnp.max(new_scores, axis=1, keepdims=True)
        )
        weights = jnp.exp(scores - top)
        new_weights = jnp.exp(new_scores - top)
        total = jnp.sum(weights, axis=1, keepdims=True)
        total = total + jnp.sum(new_weights, axis=1, keepdims=True)
        inverse = 1.0 / total
        result = dot((weights * inverse).astype(bf16), held[:, HEAD:])
        result = result + dot((new_weights * inverse).astype(bf16), new[:, HEAD:])
        for step in range(2):
            for head in range(2):
                first = (step * 2 + head) * ROWS
                out[
                    step * 128 + at : step * 128 + at + ROWS, head * HEAD : (head + 1) * HEAD
                ] = result[first : first + ROWS].astype(bf16)


def columns(k, other):
    def view(ref, order):
        place = order[k] >> 1 if other else order[k]
        return ref.at[:, pl.ds(pl.multiple_of(place * 512, 512), 512)]

    return view


def columns_of(weights, k):
    return [(w, (256, 512), columns(k, i == 1)) for i, w in enumerate(weights)]


def gather_blocks(shapes, places, scalar, *arrays, moved):
    count = len(arrays)

    def body(*refs):
        outs, sems = refs[1 + count : -1], refs[-1]
        copies = [
            pltpu.make_async_copy(view(refs[1 + i], refs[0]), outs[o].at[index], sems.at[n])
            for n, (i, view, o, index) in enumerate(places)
        ]
        for copy in copies:
            copy.start()
        for copy in copies:
            copy.wait()

    return pl.pallas_call(
        body,
        in_specs=[SMEM] + [HBM] * count,
        out_specs=[VMEM] * len(shapes),
        out_shape=[jax.ShapeDtypeStruct(shape, bf16) for shape in shapes],
        scratch_shapes=[pltpu.SemaphoreType.DMA((len(places),))],
        cost_estimate=pl.CostEstimate(flops=0, bytes_accessed=moved, transcendentals=0),
        compiler_params=pltpu.CompilerParams(vmem_limit_bytes=LARGE),
    )(scalar, *arrays)


def project_far(mine, other, weight, down, down_other, right, left, low):
    inner = dot(mine[...], down[...], ((1,), (1,))) + dot(
        other[...], down_other[...], ((1,), (1,))
    )
    packed = jnp.concatenate([inner[32 * i : 32 * i + 32] for i in range(8)], axis=1)
    low[...] = packed
    right[128:] = packed.astype(bf16)
    left[128:] = packed.astype(bf16)
    both = jnp.concatenate([mine[...], other[...]], axis=1)
    result = dot(both, weight[0])
    right[:128] = result[:128].astype(bf16)
    left[:128] = result[128:].astype(bf16)


def project_near(mine, other, weight, *targets):
    both = jnp.concatenate([mine[...], other[...]], axis=1)
    for i, target in enumerate(targets):
        target[...] = dot(both, weight[i])


def project_later(mine, other, weight, right, left, *targets):
    both = jnp.concatenate([mine[...], other[...]], axis=1)
    result = dot(both, weight[0])
    right[...] = result[:128].astype(bf16)
    left[...] = result[128:].astype(bf16)
    for i, target in enumerate(targets):
        target[...] = dot(both, weight[i + 1])


def forward(right, left, from_left, from_right, go_right, go_left):
    go_right[:128] = (right[:128] + from_left[:128].astype(f32)).astype(bf16)
    go_right[128:256] = right[128:].astype(bf16)
    go_left[:128] = left[:128].astype(bf16)
    go_left[128:256] = (left[128:] + from_right[:128].astype(f32)).astype(bf16)
    if go_right.shape[0] > 256:
        go_right[256:] = from_left[128:]
        go_left[256:] = from_right[128:]


def add_x(keep, low, from_left, from_right, far_left, far_right, message):
    message[:256] = (
        keep[...] + far_left[:256].astype(f32) + far_right[:256].astype(f32)
    ).astype(bf16)
    message[256:] = (
        low[...]
        + from_left[128:].astype(f32)
        + from_right[128:].astype(f32)
        + far_left[256:].astype(f32)
    ).astype(bf16)


def own_part(keep, far_left, far_right, hidden, out):
    out[...] = (
        hidden[...].astype(f32)
        + keep[...]
        + far_left[...].astype(f32)
        + far_right[...].astype(f32)
    )


def finish(own, message, from_z, out_up, out):
    packed = (message[256:].astype(f32) + from_z[256:].astype(f32)).astype(bf16)
    inner = stacked([packed[:, 64 * i : 64 * i + 64] for i in range(8)])
    out[...] = (
        own[...] + from_z[:256].astype(f32) + 0.5 * dot(inner, out_up[...])
    ).astype(bf16)


def on_device(
    hidden,
    query_base_weight,
    output_base_weight,
    cache,
    fresh,
    lengths,
    grad_query_down,
    grad_query_up,
    grad_output_down,
    grad_output_up,
    *state,
):
    rank = lax.axis_index("tp")
    core = rank % 2
    z_hi = (rank // 2) % 2
    x = rank // 4

    steps = jnp.arange(8, dtype=jnp.int32)
    order = ((x + steps // 2) % 4) * 4 + (z_hi ^ (steps % 2)) * 2 + core

    gradient = call(
        pack_gradients,
        [((N, 48, HEAD), f32)],
        fetch=(grad_query_down, grad_query_up, grad_output_down, grad_output_up),
    )
    parts = lax.all_to_all(gradient, "rep", 0, 0)

    hidden = hidden.reshape(256, 512)
    left = to_right(hidden)
    right = to_left(hidden)
    across = to_across(hidden)
    held = call(pack_state, [((1, 144, HEAD), bf16)], fetch=state)
    held = both_of(held, 1)
    held = both_of(held, 2)

    summed, message = call(
        sum_gradients,
        [((4, 1536), f32), ((N, 64, HEAD), bf16)],
        parts,
        tokens=(left, right, across, held),
        moved=CHAIN,
        limit=SMALL,
    )
    all_parts = lax.all_to_all(message, "rep", 0, 0)
    held = both_of(held, 4)

    squares_sent = call(
        column_squares,
        [((N, 8, HEAD), f32)],
        all_parts,
        moved=CHAIN,
        limit=SMALL,
    )
    squares = lax.all_to_all(squares_sent, "tp", 0, 0)
    zed = to_z(join((256, 512), [(0, ALL, ALL)], hidden, token=summed))
    held_far = to_replica(held, 8)
    set_h = along_x(hidden, right, across, left)
    set_h_other = to_core(set_h)

    def given(k):
        return lambda ref, core: ref.at[
            :, pl.ds(pl.multiple_of((2 * k + 1 - core[0]) * 512, 512), 512)
        ]

    (give,) = gather_blocks(
        [(256, 4096)],
        [(0, given(k), 0, (slice(None), pl.ds(512 * k, 512))) for k in range(8)],
        core.reshape(1),
        output_base_weight,
        moved=4 << 20,
    )
    weights = (output_base_weight, to_core(give))
    used = ((5,), (3, 7), (4, 1, 2, 6, 0))
    counts = tuple(map(len, used))
    w_far, w_near, w_later = gather_blocks(
        [(count, 512, 512) for count in counts],
        [
            (i, columns(k, i == 1), o, (n, pl.ds(256 * i, 256)))
            for o, ks in enumerate(used)
            for n, k in enumerate(ks)
            for i in range(2)
        ],
        order,
        *weights,
        moved=8 << 20,
    )

    message, up, out_down, out_up = call(
        make_copies,
        [((N, 128, HEAD), bf16), ((64, 256), bf16), ((64, 256), bf16), ((64, 512), bf16)],
        lax.axis_index("rep").reshape(1),
        scalars=1,
        fetch=(hidden,),
        take=(squares, all_parts, held, held_far),
        moved=CHAIN,
        room=[pltpu.VMEM((N, 48, HEAD), f32)],
    )
    lows = lax.all_to_all(message, "tp", 0, 0)
    out_down_other = to_core(out_down)
    updated = call(
        update_state,
        [((4, w), f32) for _ in range(3) for w in WIDTHS],
        squares,
        fetch=state,
        take=(summed,),
    )
    set_z = along_x(zed, to_left(zed), to_across(zed), to_right(zed))
    set_z_other = to_core(set_z)
    base = call(
        base_queries,
        [((256, 256), f32)],
        order,
        scalars=1,
        fetch=(query_base_weight,),
        take=(set_h, set_h_other, set_z, set_z_other),
        flops=2 * 256 * 8192 * 256,
        moved=8 << 20,
    )

    frequency = jnp.power(rope_base, -2.0 * jnp.arange(64, dtype=f32) / HEAD)
    positions = (lengths[None, :] + jnp.arange(2, dtype=jnp.int32)[:, None]).astype(f32)
    angles = positions[:, :, None] * frequency
    cosine = jnp.cos(angles)
    sine = jnp.sin(angles)
    tables = jnp.concatenate(
        [
            jnp.concatenate([cosine, cosine], axis=2),
            jnp.concatenate([-sine, sine], axis=2),
            jnp.broadcast_to(lengths.astype(f32)[None, :, None], (1, 128, HEAD)),
        ]
    )
    attended = call(
        attention,
        [((256, 256), bf16)],
        lows,
        base,
        up,
        tables,
        cache.reshape(4096, 256),
        fresh.reshape(256, 256),
        tokens=(w_far,),
        limit=SMALL,
        flops=2 * 512 * 512 * 256,
        moved=4 << 20,
    )

    attended_other = to_core(attended)
    far_right, far_left, low = call(
        project_far,
        [((160, 512), bf16), ((160, 512), bf16), ((32, 512), f32)],
        attended,
        attended_other,
        w_far,
        out_down,
        out_down_other,
        limit=SMALL,
        flops=2 * 256 * 512 * 512,
        moved=1 << 20,
    )
    from_left = to_right(far_right)
    from_right = to_left(far_left)
    near_right, near_left = call(
        project_near,
        [((256, 512), f32)] * 2,
        attended,
        attended_other,
        w_near,
        limit=SMALL,
        flops=2 * 256 * 512 * 1024,
        moved=2 << 20,
    )
    later_right, later_left, keep, later_near_right, later_near_left, later_keep = call(
        project_later,
        [((128, 512), bf16)] * 2 + [((256, 512), f32)] * 4,
        attended,
        attended_other,
        w_later,
        limit=SMALL,
        flops=2 * 256 * 512 * 2560,
        moved=5 << 20,
    )
    later_from_left = to_right(later_right)
    later_from_right = to_left(later_left)
    go_right, go_left = call(
        forward,
        [((288, 512), bf16)] * 2,
        near_right,
        near_left,
        from_left,
        from_right,
        limit=SMALL,
    )
    got_left = to_right(go_right)
    got_right = to_left(go_left)
    later_go_right, later_go_left = call(
        forward,
        [((256, 512), bf16)] * 2,
        later_near_right,
        later_near_left,
        later_from_left,
        later_from_right,
        limit=SMALL,
    )
    later_got_left = to_right(later_go_right)
    later_got_right = to_left(later_go_left)
    message = call(
        add_x,
        [((288, 512), bf16)],
        keep,
        low,
        from_left,
        from_right,
        got_left,
        got_right,
        limit=SMALL,
    )
    from_z = to_z(message)
    own = call(
        own_part,
        [((256, 512), f32)],
        later_keep,
        later_got_left,
        later_got_right,
        fetch=(hidden,),
        limit=SMALL,
    )
    decoded = call(
        finish, [((256, 512), bf16)], own, message, from_z, take=(out_up,), limit=SMALL
    )
    return (decoded.reshape(2, 128, 512), *updated)


def solution(mesh):
    return jax.shard_map(
        on_device,
        mesh=mesh,
        in_specs=(
            P(None, "rep", "tp"),
            P(None, "tp"),
            P("tp", None),
            P("rep", "tp", None, None),
            P("rep", "tp", None, None),
            P("rep"),
        )
        + (P("rep", None, "tp"),) * 4
        + (P("rep", "tp"),) * 12,
        out_specs=(P(None, "rep", "tp"),) + (P("rep", "tp"),) * 12,
        check_vma=False,
    )
```
